32 devices in a mesh: row: 4 (over y, x), col: 8 (over z, core).
Axes of the slice: x: 2, y: 2, z: 4, core: 2. Of those that a mesh axis runs over, the one named last changes fastest.
Arguments:
- upper_blocks: bfloat16 [4, 8, 63, 128, 128], P('row', 'col'), may hold values from -1.5 to 1.5
- block_targets: int32 [4, 8, 63], P('row', 'col'), may hold values from 0 to 7, as said below
- product_plan: int32 [4, 8, 2, 128, 3], P('row', 'col'), may hold values from 0 to 125, as said below
- live_counts: int32 [4, 8, 2], P('row', 'col'), may hold values from 24 to 128, as said below
Outputs:
- result_blocks: bfloat16 [4, 8, 32, 128, 128], P('row', 'col')
The draws below stay inside these ranges and needn't reach their ends.
Inputs may be any that keep to these rules, and one draw needn't show every extreme that they name: `block_targets`: A device's stored blocks never target its own column; within one grid row, the k-th stored block of every device targets the same number of columns onward, and at most 9 of a device's blocks target one column, reached in every draw. `product_plan`: columns 0 and 1 name panel blocks below 126, column 2 a result block below 32. In section 1, all 128 slots of a device together name exactly 24 distinct left blocks and exactly 24 distinct right blocks. `live_counts`: in each section some device has all 128 slots live.
All inputs are finite; a program needn't handle non-finite values.
Results may differ from the reference program's by a relative error of at most 0.008.
Values may be sent and summed in bfloat16 or wider, within the bound.
No kernel may reach another device: no remote copies, remote signals or barrier semaphores. Data moves between devices by JAX's collectives and lax.ppermute only.
A program may use at most 64 MiB of HBM per device.

```python
import jax
import jax.numpy as jnp
from jax import lax

BLOCK = 128
STORED = 63
PRODS = 128
USED = 24
OUTSLOTS = 32
N_ROW = 4
N_COL = 8


def draw_block_targets(key, part):
    key = jax.random.fold_in(key, 11)
    row_keys = jax.random.split(key, N_ROW)
    orders = jax.vmap(lambda single: jax.random.permutation(single, N_COL - 1))(row_keys)
    slot_ids = jnp.arange(STORED, dtype=jnp.int32) % (N_COL - 1)
    offsets = 1 + jnp.take(orders, slot_ids, axis=1)
    columns = jnp.arange(N_COL, dtype=jnp.int32)
    return ((columns[None, :, None] + offsets[:, None, :]) % N_COL).astype(jnp.int32)


def pick_subset(key, devices):
    first_key, second_key = jax.random.split(key)
    device_keys = jax.random.split(first_key, devices)
    orders = jax.vmap(lambda single: jax.random.permutation(single, 2 * STORED))(device_keys)[:, :USED]
    filler = jax.random.randint(second_key, (devices, PRODS), 0, USED)
    positions = jnp.arange(PRODS, dtype=jnp.int32)
    chosen = jnp.where(positions[None, :] < USED, jnp.minimum(positions, USED - 1)[None, :], filler)
    return jnp.take_along_axis(orders, chosen, axis=1).astype(jnp.int32)


def draw_product_plan(key, part):
    key = jax.random.fold_in(key, 23)
    keys = jax.random.split(key, 6)
    devices = N_ROW * N_COL
    first_left = jax.random.randint(keys[0], (devices, PRODS), 0, 2 * STORED)
    first_right = jax.random.randint(keys[1], (devices, PRODS), 0, 2 * STORED)
    first_out = jax.random.randint(keys[2], (devices, PRODS), 0, OUTSLOTS)
    first_left = first_left.at[0, 0].set(2 * STORED - 1)
    first_right = first_right.at[0, 0].set(0)
    first_out = first_out.at[0, 0].set(OUTSLOTS - 1)
    second_left = pick_subset(keys[3], devices)
    second_right = pick_subset(keys[4], devices)
    second_out = jax.random.randint(keys[5], (devices, PRODS), 0, OUTSLOTS)
    first = jnp.stack([first_left, first_right, first_out], axis=-1)
    second = jnp.stack([second_left, second_right, second_out], axis=-1)
    plan = jnp.stack([first, second], axis=1)
    return plan.reshape(N_ROW, N_COL, 2, PRODS, 3).astype(jnp.int32)


def draw_live_counts(key, part):
    key = jax.random.fold_in(key, 37)
    keys = jax.random.split(key, 3)
    devices = N_ROW * N_COL
    first = jax.random.randint(keys[0], (devices, 2), 0, PRODS + 1)
    second = jax.random.randint(keys[1], (devices, 2), 0, PRODS + 1)
    counts = jnp.maximum(jnp.minimum(first, second), USED)
    busiest = jax.random.randint(keys[2], (2,), 0, devices)
    device_ids = jnp.arange(devices, dtype=jnp.int32)
    counts = jnp.where(device_ids[:, None] == busiest[None, :], PRODS, counts)
    return counts.reshape(N_ROW, N_COL, 2).astype(jnp.int32)


def steps_of(rng, shape, pieces, least, largest):
    loudness = 1.0
    for axis_at, parts in pieces:
        draws = jax.random.uniform(jax.random.fold_in(jax.random.fold_in(rng, 6), axis_at), (parts,), jnp.float32, least / len(pieces), largest / len(pieces))
        loudness = loudness * jnp.repeat(jnp.exp(draws), shape[axis_at] // parts).reshape((-1,) + (1,) * (len(shape) - 1 - axis_at))
    return loudness


def noise(own_key, extent, scale, limit, cuts=(), kind=jnp.bfloat16):
    level = steps_of(own_key, extent, cuts, -0.22, 0.18) if cuts else 1.0
    values = jax.random.normal(own_key, extent, jnp.float32) * scale * level
    return jnp.minimum(jnp.maximum(values, -limit), limit).astype(kind)


def setup_inputs(seed: int = 0) -> dict:
    key_of = jax.random.split(jax.random.key(seed), 5)
    return {
        "upper_blocks": noise(key_of[0], (N_ROW, N_COL, STORED, BLOCK, BLOCK), 0.25, 1.5, ((0, 4), (1, 8))),
        "block_targets": draw_block_targets(jax.random.fold_in(key_of[4], 71), 0),
        "product_plan": draw_product_plan(jax.random.fold_in(key_of[4], 71), 0),
        "live_counts": draw_live_counts(jax.random.fold_in(key_of[4], 71), 0),
    }


def section_terms(left_panel, right_panel, left_index, right_index, out_index, count):
    left_rows = jnp.take(left_panel, left_index, axis=0).astype(jnp.float32)
    right_rows = jnp.take(right_panel, right_index, axis=0).astype(jnp.float32)
    terms = jnp.einsum('pij,pjk->pik', left_rows, right_rows, precision=lax.Precision.HIGHEST)
    alive = (jnp.arange(left_index.shape[0], dtype=jnp.int32) < count).astype(jnp.float32)
    return jax.ops.segment_sum(terms * alive[:, None, None], out_index, num_segments=OUTSLOTS)


def reference(upper_blocks, block_targets, product_plan, live_counts):
    columns = jnp.arange(N_COL, dtype=jnp.int32)
    grid_rows = jnp.arange(N_ROW, dtype=jnp.int32)
    offsets = (block_targets - columns[None, :, None]) % N_COL
    sources = (columns[None, :, None] - offsets) % N_COL
    picked = upper_blocks[grid_rows[:, None, None], sources, jnp.arange(STORED, dtype=jnp.int32)[None, None, :]]
    panels = jnp.concatenate([upper_blocks, jnp.swapaxes(picked, -1, -2)], axis=2)

    def one_device(index):
        grid_row = index // N_COL
        grid_col = index % N_COL
        own_panel = panels[grid_row, grid_col]
        left_panel = panels[grid_row, (grid_col + 1) % N_COL]
        right_panel = panels[(grid_row + 1) % N_ROW, grid_col]
        plan = product_plan[grid_row, grid_col]
        counts = live_counts[grid_row, grid_col]
        total = section_terms(own_panel, own_panel, plan[0, :, 0], plan[0, :, 1], plan[0, :, 2], counts[0])
        total = total + section_terms(left_panel, right_panel, plan[1, :, 0], plan[1, :, 1], plan[1, :, 2], counts[1])
        return total.astype(jnp.bfloat16)

    result = lax.map(one_device, jnp.arange(N_ROW * N_COL, dtype=jnp.int32))
    return result.reshape(N_ROW, N_COL, OUTSLOTS, BLOCK, BLOCK)
```

```python
import functools

import jax
import jax.numpy as jnp
from jax import lax
from jax.experimental import pallas as pl
from jax.experimental.pallas import tpu as pltpu
from jax.sharding import PartitionSpec as P

OUTSLOTS = 32
USED = 24
UNROLL = 4
MIB = 1 << 20

SMEM = pl.BlockSpec(memory_space=pltpu.SMEM)
VMEM = pl.BlockSpec(memory_space=pltpu.VMEM)
HBM = pl.BlockSpec(memory_space=pltpu.HBM)


def i32(*shape):
    return jax.ShapeDtypeStruct(shape, jnp.int32)


def params(mib):
    return pltpu.CompilerParams(vmem_limit_bytes=mib * MIB)


def moved(value, axis, steps):
    count = lax.axis_size(axis)
    return lax.ppermute(value, axis, [(s, (s + steps) % count) for s in range(count)])


def after(value, *needed):
    return lax.optimization_barrier((value, *needed))[0]


class Layout:
    def __init__(self, stored, cols):
        self.stored = stored
        self.cols = cols
        self.cap = (stored + cols - 2) // (cols - 1)
        others = list(range(2, cols))
        half = cols // 2
        others.sort(key=lambda d: (half - abs(d - half), d))
        pieces = min(6, len(others))
        cuts = [len(others) * i // pieces for i in range(pieces + 1)]
        self.stages = [others[a:b] for a, b in zip(cuts, cuts[1:])] + [[1]]
        self.base = [0] * cols
        self.start = []
        at = 0
        for stage in self.stages:
            self.start.append(at)
            for d in stage:
                self.base[d] = at
                at += self.cap
        self.total = at
        self.start.append(at)

    def size(self, s):
        return self.start[s + 1] - self.start[s]


def sort_kernel(lay, tgt, col, stored_ref, out, pos, inv, buf, cnt, sem):
    me = col[0]
    for d in range(lay.cols):
        cnt[d] = lay.base[d]

    def place(k, carry):
        d = tgt[k] - me
        d = jnp.where(d < 0, d + lay.cols, d)
        q = cnt[d]
        cnt[d] = q + 1
        pos[k] = q
        inv[q] = k
        return carry

    lax.fori_loop(0, lay.stored, place, 0)
    n = lay.size(0)

    def fetch(j, carry):
        pltpu.make_async_copy(stored_ref.at[inv[j]], buf.at[j], sem).start()
        return carry

    lax.fori_loop(0, n, fetch, 0)
    pltpu.make_async_copy(buf, buf, sem).wait()

    def flip(j, carry):
        out[j] = buf[j].T
        return carry

    lax.fori_loop(0, n, flip, 0)


def first_stage(lay, targets, col, stored):
    block = stored.shape[-1]
    n = lay.size(0)
    return pl.pallas_call(
        functools.partial(sort_kernel, lay),
        out_shape=(jax.ShapeDtypeStruct((n, block, block), stored.dtype), i32(lay.stored), i32(lay.total)),
        in_specs=[SMEM, SMEM, HBM],
        out_specs=(VMEM, SMEM, SMEM),
        scratch_shapes=[
            pltpu.VMEM((n, block, block), stored.dtype),
            pltpu.SMEM((lay.cols,), jnp.int32),
            pltpu.SemaphoreType.DMA,
        ],
        compiler_params=params(8),
        name="sort_first",
    )(targets, col, stored)


def rest_kernel(lay, inv, stored_ref, *outs):
    for s in range(1, len(lay.stages)):

        def flip(j, carry, s=s):
            outs[s - 1][j] = stored_ref[inv[lay.start[s] + j]].T
            return carry

        lax.fori_loop(0, lay.size(s), flip, 0)


def rest_stages(lay, inv, stored):
    block = stored.shape[-1]
    shapes = tuple(
        jax.ShapeDtypeStruct((lay.size(s), block, block), stored.dtype) for s in range(1, len(lay.stages))
    )
    return pl.pallas_call(
        functools.partial(rest_kernel, lay),
        out_shape=shapes,
        in_specs=[SMEM, VMEM],
        out_specs=(VMEM,) * len(shapes),
        compiler_params=params(12),
        name="flip_rest",
    )(inv, stored)


def wanted_kernel(prods, plan, reqs_l, reqs_r, slots_l, slots_r, seen):
    for side, (reqs, slots) in enumerate(((reqs_l, slots_l), (reqs_r, slots_r))):

        def clear(i, carry):
            seen[i] = -1
            return carry

        lax.fori_loop(0, seen.shape[0], clear, 0)

        def clear_request(i, carry, reqs=reqs):
            reqs[i] = 0
            return carry

        lax.fori_loop(0, USED, clear_request, 0)

        def step(p, n, side=side, reqs=reqs, slots=slots):
            which = plan[side * prods + p]
            known = seen[which]
            fresh = known < 0
            slot = jnp.where(fresh, n, known)
            seen[which] = slot
            reqs[slot] = which
            slots[p] = slot
            return jnp.where(fresh, n + 1, n)

        lax.fori_loop(0, prods, step, 0)


def wanted(panel_size, plan_flat, prods):
    return pl.pallas_call(
        functools.partial(wanted_kernel, prods),
        out_shape=(i32(USED), i32(USED), i32(prods), i32(prods)),
        in_specs=[SMEM],
        out_specs=(SMEM,) * 4,
        scratch_shapes=[pltpu.SMEM((panel_size,), jnp.int32)],
        name="wanted",
    )(plan_flat)


def pick_kernel(lay, stages, req, pos, stored_ref, *rest):
    parts, out = rest[: len(stages)], rest[len(stages)]

    def step(n, carry):
        which = req[n]
        lower = which >= lay.stored
        q = pos[jnp.where(lower, which - lay.stored, 0)]

        @pl.when(jnp.logical_not(lower))
        def _():
            out[n] = stored_ref[which]

        for s, part in zip(stages, parts):

            @pl.when(lower & (q >= lay.start[s]) & (q < lay.start[s + 1]))
            def _(s=s, part=part):
                out[n] = part[q - lay.start[s]]

        return carry

    lax.fori_loop(0, USED, step, 0)


def pick(lay, stages, req, pos, stored, parts, name):
    block = stored.shape[-1]
    return pl.pallas_call(
        functools.partial(pick_kernel, lay, stages),
        out_shape=jax.ShapeDtypeStruct((USED, block, block), stored.dtype),
        in_specs=[SMEM, SMEM, VMEM] + [VMEM] * len(parts),
        out_specs=VMEM,
        compiler_params=params(16),
        name=name,
    )(req, pos, stored, *parts)


def multiply(count, entry, left, right, acc):
    spare = acc.shape[0] - 1

    def group(g, carry):
        found = []
        for u in range(UNROLL):
            p = g * UNROLL + u
            i, j, o = entry(p)
            o = jnp.where(p < count, o, spare)
            found.append((o, jnp.dot(left[i], right[j], preferred_element_type=jnp.float32)))
        for o, term in found:
            acc[o] += term
        return carry

    lax.fori_loop(0, (count + UNROLL - 1) // UNROLL, group, 0)


def own_kernel(lay, prods, plan, counts, pos, stored_ref, *rest):
    parts = rest[: len(lay.stages)]
    acc, panel, sem = rest[len(lay.stages) :]
    copies = [pltpu.make_async_copy(stored_ref, panel.at[pl.ds(0, lay.stored)], sem.at[0])]
    for s, part in enumerate(parts):
        copies.append(
            pltpu.make_async_copy(part, panel.at[pl.ds(lay.stored + lay.start[s], lay.size(s))], sem.at[s + 1])
        )
    for copy in copies:
        copy.start()

    def zero(o, carry):
        acc[o] = jnp.zeros(acc.shape[1:], acc.dtype)
        return carry

    lax.fori_loop(0, acc.shape[0], zero, 0)
    for copy in copies:
        copy.wait()

    def where(which):
        lower = which >= lay.stored
        return jnp.where(lower, lay.stored + pos[jnp.where(lower, which - lay.stored, 0)], which)

    def entry(p):
        return where(plan[p]), where(plan[prods + p]), plan[2 * prods + p]

    multiply(counts[0], entry, panel, panel, acc)


def own_section(lay, plan_flat, counts, pos, stored, parts):
    block = stored.shape[-1]
    prods = plan_flat.shape[0] // 3
    return pl.pallas_call(
        functools.partial(own_kernel, lay, prods),
        out_shape=jax.ShapeDtypeStruct((OUTSLOTS + 1, block, block), jnp.float32),
        in_specs=[SMEM, SMEM, SMEM, VMEM] + [VMEM] * len(parts),
        out_specs=VMEM,
        scratch_shapes=[
            pltpu.VMEM((lay.stored + lay.total, block, block), stored.dtype),
            pltpu.SemaphoreType.DMA((len(parts) + 1,)),
        ],
        compiler_params=params(20),
        name="own_section",
    )(plan_flat, counts, pos, stored, *parts)


def next_kernel(lay, late, prods, plan, counts, slots_l, slots_r, pos, pos_r, acc, left_ref, self_ref, right_ref, *rest):
    parts = rest[: len(late)]
    out, left, right, sem = rest[len(late) :]
    copies = [
        pltpu.make_async_copy(left_ref, left.at[pl.ds(0, USED)], sem.at[0]),
        pltpu.make_async_copy(self_ref, left.at[pl.ds(USED, self_ref.shape[0])], sem.at[1]),
        pltpu.make_async_copy(right_ref, right.at[pl.ds(0, USED)], sem.at[2]),
    ]
    late_from = lay.start[late[0]] if late else lay.total
    for n, (s, part) in enumerate(zip(late, parts)):
        at = USED + lay.start[s] - late_from
        copies.append(pltpu.make_async_copy(part, right.at[pl.ds(at, lay.size(s))], sem.at[3 + n]))
    for copy in copies:
        copy.start()
    for copy in copies:
        copy.wait()
    self_from = lay.start[-2]

    def where(which, slot, table, first):
        lower = which >= lay.stored
        q = table[jnp.where(lower, which - lay.stored, 0)]
        return jnp.where(lower & (q >= first), USED + q - first, slot)

    def entry(p):
        i = where(plan[p], slots_l[p], pos, self_from)
        j = where(plan[prods + p], slots_r[p], pos_r, late_from)
        return i, j, plan[2 * prods + p]

    multiply(counts[1], entry, left, right, acc)

    def finish(o, carry):
        out[o] = acc[o].astype(out.dtype)
        return carry

    lax.fori_loop(0, OUTSLOTS, finish, 0)


def next_section(lay, late, plan_flat, counts, slots_l, slots_r, pos, pos_r, acc, left, self_part, right, parts):
    block = left.shape[-1]
    prods = plan_flat.shape[0] // 3
    late_size = sum(lay.size(s) for s in late)
    return pl.pallas_call(
        functools.partial(next_kernel, lay, late, prods),
        out_shape=jax.ShapeDtypeStruct((OUTSLOTS, block, block), left.dtype),
        in_specs=[SMEM] * 6 + [VMEM] * (4 + len(parts)),
        out_specs=VMEM,
        scratch_shapes=[
            pltpu.VMEM((USED + self_part.shape[0], block, block), left.dtype),
            pltpu.VMEM((USED + late_size, block, block), left.dtype),
            pltpu.SemaphoreType.DMA((3 + len(parts),)),
        ],
        compiler_params=params(20),
        name="next_section",
    )(plan_flat, counts, slots_l, slots_r, pos, pos_r, acc, left, self_part, right, *parts)


FLIGHT = 3
EARLY = 7


def body(upper_blocks, block_targets, product_plan, live_counts):
    stored = upper_blocks[0, 0]
    counts = live_counts[0, 0]
    plan = jnp.swapaxes(product_plan[0, 0], 1, 2)
    prods = plan.shape[2]
    plans = plan.reshape(2, 3 * prods)
    lay = Layout(stored.shape[0], lax.axis_size("col"))
    stages = range(len(lay.stages))
    early = list(stages)[:EARLY]
    late = list(stages)[EARLY:]
    col = lax.axis_index("col").astype(jnp.int32).reshape(1)

    first, pos, inv = first_stage(lay, block_targets[0, 0], col, stored)

    def exchange(s, send):
        parts = [
            moved(send[n * lay.cap : (n + 1) * lay.cap], "col", d) for n, d in enumerate(lay.stages[s])
        ]
        return parts[0] if len(parts) == 1 else jnp.concatenate(parts, axis=0)

    got = [exchange(0, first)]
    sends = [first, *rest_stages(lay, inv, stored)]
    reqs_l, reqs_r, slots_l, slots_r = wanted(2 * lay.stored, after(plans[1], got[0]), prods)
    asked_l = moved(reqs_l, "col", 1)
    asked_r = moved(reqs_r, "row", 1)
    pos_r = moved(pos, "row", -1)
    for s in stages[1:]:
        send = sends[s] if s < FLIGHT else after(sends[s], got[s - FLIGHT])
        got.append(exchange(s, send))
    right = moved(pick(lay, early, asked_r, pos, stored, [got[s] for s in early], "pick_right"), "row", -1)
    forwarded = [moved(got[s], "row", -1) for s in late]
    ready = list(stages)[:-1]
    left = moved(pick(lay, ready, asked_l, pos, stored, [got[s] for s in ready], "pick_left"), "col", -1)
    acc = own_section(lay, plans[0], counts, pos, stored, got)
    out = next_section(
        lay, late, plans[1], counts, slots_l, slots_r, pos, pos_r, acc, left, sends[-1], right, forwarded
    )
    return out[None, None]


def solution(mesh):
    placed = (
        P("row", "col", None, None, None),
        P("row", "col", None),
        P("row", "col", None, None, None),
        P("row", "col", None),
    )
    return jax.shard_map(
        body,
        mesh=mesh,
        in_specs=placed,
        out_specs=P("row", "col", None, None, None),
        check_vma=False,
    )
```

```python
import functools

import jax
import jax.numpy as jnp
from jax import lax
from jax.experimental import pallas as pl
from jax.experimental.pallas import tpu as pltpu
from jax.sharding import PartitionSpec as P

OUTSLOTS = 32
USED = 24
UNROLL = 8
FIRST = 2
LEFT_PIECES = 1
RIGHT_PIECES = 1
FIRST_MIB = 62
MIB = 1 << 20

SMEM = pl.BlockSpec(memory_space=pltpu.SMEM)
VMEM = pl.BlockSpec(memory_space=pltpu.VMEM)
HBM = pl.BlockSpec(memory_space=pltpu.HBM)


def cost(us):
    return pl.CostEstimate(flops=0, bytes_accessed=int(us * 3.5e6), transcendentals=0)


def i32(*shape):
    return jax.ShapeDtypeStruct(shape, jnp.int32)


def params(mib):
    return pltpu.CompilerParams(vmem_limit_bytes=mib * MIB)


def moved(value, axis, steps):
    count = lax.axis_size(axis)
    return lax.ppermute(value, axis, [(s, (s + steps) % count) for s in range(count)])


def after(value, *needed):
    return lax.optimization_barrier((value, *needed))[0]


class Order:
    def __init__(self, token):
        self.token = token

    def gate(self, value):
        value, self.token = lax.optimization_barrier((value, self.token))
        return value


class Layout:
    def __init__(self, stored, cols):
        self.stored = stored
        self.cols = cols
        self.cap = (stored + cols - 2) // (cols - 1)
        half = cols // 2
        others = [d for d in range(2, cols) if d != half]
        others.sort(key=lambda d: (half - abs(d - half), d))
        others = others[1:3] + others[:1] + others[3:]
        pieces = min(5, len(others))
        cuts = [len(others) * i // pieces for i in range(pieces + 1)]
        self.stages = [others[a:b] for a, b in zip(cuts, cuts[1:])] + [[1], [half]]
        self.base = [0] * cols
        self.start = []
        at = 0
        for stage in self.stages:
            self.start.append(at)
            for d in stage:
                self.base[d] = at
                at += self.cap
        self.total = at
        self.start.append(at)
        self.self_stage = self.stages.index([1])

    def size(self, s):
        return self.start[s + 1] - self.start[s]


def offset_of(lay, tgt, k, me):
    d = tgt[k] - me
    return jnp.where(d < 0, d + lay.cols, d)


def first_kernel(lay, tgt, col, stored_ref, *rest):
    outs, (buf, found, sem) = rest[:FIRST], rest[FIRST:]
    goals = []
    for n, offset in enumerate(d for stage in lay.stages[:FIRST] for d in stage):
        goal = col[0] + offset
        goals.append(jnp.where(goal >= lay.cols, goal - lay.cols, goal))
    at = [jnp.int32(n * lay.cap) for n in range(len(goals))]
    for k in range(lay.stored):
        target = tgt[k]
        for n, goal in enumerate(goals):
            hit = target == goal
            found[jnp.where(hit, at[n], lay.total)] = k
            at[n] = at[n] + hit.astype(jnp.int32)
    total = lay.start[FIRST]
    for j in range(total):
        pltpu.make_async_copy(stored_ref.at[found[j]], buf.at[j], sem).start()
    pltpu.make_async_copy(buf, buf, sem).wait()
    for s, out in enumerate(outs):
        for j in range(lay.size(s)):
            out[j] = buf[lay.start[s] + j].T


def first_stage(lay, targets, col, stored):
    block = stored.shape[-1]
    return pl.pallas_call(
        functools.partial(first_kernel, lay),
        out_shape=tuple(jax.ShapeDtypeStruct((lay.size(s), block, block), stored.dtype) for s in range(FIRST)),
        in_specs=[SMEM, SMEM, HBM],
        out_specs=(VMEM,) * FIRST,
        scratch_shapes=[
            pltpu.VMEM((lay.start[FIRST], block, block), stored.dtype),
            pltpu.SMEM((lay.total + 1,), jnp.int32),
            pltpu.SemaphoreType.DMA,
        ],
        compiler_params=params(FIRST_MIB),
        name="first_stage",
    )(targets, col, stored)


def rest_kernel(lay, tgt, col, ids, stored_ref, *rest):
    outs, pos, inv, cnt = rest[:-3], rest[-3], rest[-2], rest[-1]
    for d in range(lay.cols):
        cnt[d] = lay.base[d]

    def place(k, carry):
        d = offset_of(lay, tgt, k, col[0])
        q = cnt[d]
        cnt[d] = q + 1
        pos[k] = q
        inv[q] = k
        return carry

    lax.fori_loop(0, lay.stored, place, 0)
    for s in range(FIRST, len(lay.stages)):

        def flip(j, carry, s=s):
            outs[s - FIRST][j] = stored_ref[inv[lay.start[s] + j]].T
            return carry

        lax.fori_loop(0, lay.size(s), flip, 0, unroll=lay.size(s) % 3 == 0 and 3 or 1)
    note = outs[lay.self_stage - FIRST]
    rows, block = ids.shape
    for row in range(rows):
        line = ids[row : row + 1, :].astype(jnp.float32)
        note[lay.size(lay.self_stage), row * 16 : row * 16 + 16, :] = jnp.broadcast_to(line, (16, block)).astype(note.dtype)


def rest_stages(lay, targets, col, ids, stored):
    block = stored.shape[-1]
    shapes = tuple(
        jax.ShapeDtypeStruct((lay.size(s) + (s == lay.self_stage), block, block), stored.dtype)
        for s in range(FIRST, len(lay.stages))
    )
    return pl.pallas_call(
        functools.partial(rest_kernel, lay),
        out_shape=shapes + (i32(lay.stored),),
        in_specs=[SMEM, SMEM, VMEM, VMEM],
        out_specs=(VMEM,) * len(shapes) + (SMEM,),
        scratch_shapes=[pltpu.SMEM((lay.total,), jnp.int32), pltpu.SMEM((lay.cols,), jnp.int32)],
        compiler_params=params(12),
        cost_estimate=cost(0.01),
        name="rest_stages",
    )(targets, col, ids, stored)


def wanted_kernel(prods, plan, reqs_r, slots_l, slots_r, seen_l, seen_r):
    def clear(i, carry):
        seen_l[i] = -1
        seen_r[i] = -1
        return carry

    lax.fori_loop(0, seen_l.shape[0], clear, 0, unroll=6 if seen_l.shape[0] % 6 == 0 else 1)
    for i in range(USED):
        reqs_r[i] = 0

    def step(p, counts):
        sides = ((slots_l, seen_l), (slots_r, seen_r))
        found = [plan[side * prods + p] for side in range(2)]
        known = [seen[which] for (_, seen), which in zip(sides, found)]
        slot = [jnp.where(k < 0, n, k) for k, n in zip(known, counts)]
        for (slots, seen), which, at in zip(sides, found, slot):
            seen[which] = at
            slots[p] = at
        reqs_r[slot[1]] = found[1]
        return tuple(n + (k < 0).astype(jnp.int32) for k, n in zip(known, counts))

    lax.fori_loop(0, prods, step, (jnp.int32(0), jnp.int32(0)), unroll=4)


def wanted(panel_size, plan_flat, prods):
    return pl.pallas_call(
        functools.partial(wanted_kernel, prods),
        out_shape=(i32(USED), i32(prods), i32(prods)),
        in_specs=[SMEM],
        out_specs=(SMEM,) * 3,
        scratch_shapes=[pltpu.SMEM((panel_size,), jnp.int32)] * 2,
        cost_estimate=cost(0.01),
        name="wanted",
    )(plan_flat)


def asked_kernel(ids, reqs, seen):
    def clear(i, carry):
        seen[i] = 0
        return carry

    lax.fori_loop(0, seen.shape[0], clear, 0, unroll=6 if seen.shape[0] % 6 == 0 else 1)

    def step(p, n):
        which = ids[p]
        known = seen[which]
        reqs[n] = which
        seen[which] = 1
        return n + 1 - known

    lax.fori_loop(0, ids.shape[0], step, jnp.int32(0), unroll=4)


def asked(panel_size, ids):
    return pl.pallas_call(
        asked_kernel,
        out_shape=i32(USED + 1),
        in_specs=[SMEM],
        out_specs=SMEM,
        scratch_shapes=[pltpu.SMEM((panel_size,), jnp.int32)],
        name="asked",
    )(ids)


def pick_kernel(lay, stages, pieces, req, pos, stored_ref, *rest):
    parts, outs = rest[: len(stages)], rest[len(stages) :]
    size = USED // pieces
    for piece, out in enumerate(outs):

        def step(n, carry, piece=piece, out=out):
            which = req[piece * size + n]
            lower = which >= lay.stored
            q = pos[jnp.where(lower, which - lay.stored, 0)]

            @pl.when(jnp.logical_not(lower))
            def _():
                out[n] = stored_ref[which]

            for s, part in zip(stages, parts):

                @pl.when(lower & (q >= lay.start[s]) & (q < lay.start[s + 1]))
                def _(s=s, part=part):
                    out[n] = part[q - lay.start[s]]

            return carry

        lax.fori_loop(0, size, step, 0)


def pick(lay, stages, pieces, req, pos, stored, parts, name):
    block = stored.shape[-1]
    return pl.pallas_call(
        functools.partial(pick_kernel, lay, stages, pieces),
        out_shape=(jax.ShapeDtypeStruct((USED // pieces, block, block), stored.dtype),) * pieces,
        in_specs=[SMEM, SMEM, VMEM] + [VMEM] * len(parts),
        out_specs=(VMEM,) * pieces,
        compiler_params=params(16),
        name=name,
    )(req, pos, stored, *parts)


def multiply(count, entry, left, right, acc):
    spare = acc.shape[0] - 1

    def group(g, carry):
        found = []
        for u in range(UNROLL):
            p = g * UNROLL + u
            i, j, o = entry(p)
            o = jnp.where(p < count, o, spare)
            found.append((o, jnp.dot(left[i], right[j], preferred_element_type=jnp.float32)))
        for o, term in found:
            acc[o] += term
        return carry

    lax.fori_loop(0, (count + UNROLL - 1) // UNROLL, group, 0)


def own_kernel(lay, prods, plan, counts, pos, stored_ref, *rest):
    parts = rest[: len(lay.stages)]
    acc, panel, sem = rest[len(lay.stages) :]
    copies = [pltpu.make_async_copy(stored_ref, panel.at[pl.ds(0, lay.stored)], sem.at[0])]
    for s, part in enumerate(parts):
        copies.append(
            pltpu.make_async_copy(
                part.at[pl.ds(0, lay.size(s))], panel.at[pl.ds(lay.stored + lay.start[s], lay.size(s))], sem.at[s + 1]
            )
        )
    for copy in copies:
        copy.start()

    def zero(o, carry):
        acc[o] = jnp.zeros(acc.shape[1:], acc.dtype)
        return carry

    lax.fori_loop(0, acc.shape[0], zero, 0)
    for copy in copies:
        copy.wait()

    def where(which):
        lower = which >= lay.stored
        return jnp.where(lower, lay.stored + pos[jnp.where(lower, which - lay.stored, 0)], which)

    def entry(p):
        return where(plan[p]), where(plan[prods + p]), plan[2 * prods + p]

    multiply(counts[0], entry, panel, panel, acc)


def own_section(lay, plan_flat, counts, pos, stored, parts):
    block = stored.shape[-1]
    prods = plan_flat.shape[0] // 3
    return pl.pallas_call(
        functools.partial(own_kernel, lay, prods),
        out_shape=jax.ShapeDtypeStruct((OUTSLOTS + 1, block, block), jnp.float32),
        in_specs=[SMEM, SMEM, SMEM, VMEM] + [VMEM] * len(parts),
        out_specs=VMEM,
        scratch_shapes=[
            pltpu.VMEM((lay.stored + lay.total, block, block), stored.dtype),
            pltpu.SemaphoreType.DMA((len(parts) + 1,)),
        ],
        compiler_params=params(20),
        cost_estimate=cost(0.01),
        name="own_section",
    )(plan_flat, counts, pos, stored, *parts)


def next_kernel(lay, late, prods, token, plan, counts, slots_l, slots_r, pos, pos_r, acc, self_ref, *rest):
    lefts, rights, parts = rest[:LEFT_PIECES], rest[LEFT_PIECES : LEFT_PIECES + RIGHT_PIECES], rest[LEFT_PIECES + RIGHT_PIECES : -4]
    out, left, right, sem = rest[-4:]
    late_from = lay.start[late[0]] if late else lay.total
    moves = [(self_ref, left, USED, lay.size(lay.self_stage))]
    moves += [(part, left, n * part.shape[0], part.shape[0]) for n, part in enumerate(lefts)]
    moves += [(part, right, n * part.shape[0], part.shape[0]) for n, part in enumerate(rights)]
    moves += [(part, right, USED + lay.start[s] - late_from, lay.size(s)) for s, part in zip(late, parts)]
    copies = [
        pltpu.make_async_copy(part.at[pl.ds(0, size)], whole.at[pl.ds(at, size)], sem.at[n])
        for n, (part, whole, at, size) in enumerate(moves)
    ]
    for copy in copies:
        copy.start()
    for copy in copies:
        copy.wait()

    def where(which, slot, table, first, last):
        lower = which >= lay.stored
        q = table[jnp.where(lower, which - lay.stored, 0)]
        return jnp.where(lower & (q >= first) & (q < last), USED + q - first, slot)

    def entry(p):
        own = lay.self_stage
        i = where(plan[p], slots_l[p], pos, lay.start[own], lay.start[own + 1])
        j = where(plan[prods + p], slots_r[p], pos_r, late_from, lay.total)
        return i, j, plan[2 * prods + p]

    multiply(counts[1], entry, left, right, acc)

    def finish(o, carry):
        out[o] = acc[o].astype(out.dtype)
        return carry

    lax.fori_loop(0, OUTSLOTS, finish, 0)


def next_section(lay, late, token, plan_flat, counts, slots_l, slots_r, pos, pos_r, acc, left, self_part, right, parts):
    block = self_part.shape[-1]
    prods = plan_flat.shape[0] // 3
    late_size = sum(lay.size(s) for s in late)
    return pl.pallas_call(
        functools.partial(next_kernel, lay, late, prods),
        out_shape=jax.ShapeDtypeStruct((OUTSLOTS, block, block), self_part.dtype),
        in_specs=[SMEM] * 7 + [VMEM] * (2 + len(left) + len(right) + len(parts)),
        out_specs=VMEM,
        scratch_shapes=[
            pltpu.VMEM((USED + lay.size(lay.self_stage), block, block), self_part.dtype),
            pltpu.VMEM((USED + late_size, block, block), self_part.dtype),
            pltpu.SemaphoreType.DMA((1 + len(left) + len(right) + len(parts),)),
        ],
        compiler_params=params(20),
        cost_estimate=cost(0.01),
        name="next_section",
    )(token, plan_flat, counts, slots_l, slots_r, pos, pos_r, acc, self_part, *left, *right, *parts)


FLIGHT = 2
EARLY = 6


def body(upper_blocks, block_targets, product_plan, live_counts):
    stored = upper_blocks[0, 0]
    targets = block_targets[0, 0]
    counts = live_counts[0, 0]
    plan = jnp.swapaxes(product_plan[0, 0], 1, 2)
    prods = plan.shape[2]
    plans = plan.reshape(2, 3 * prods)
    lay = Layout(stored.shape[0], lax.axis_size("col"))
    stages = list(range(len(lay.stages)))
    early, late = stages[:EARLY], stages[EARLY:]
    col = lax.axis_index("col").astype(jnp.int32).reshape(1)

    def exchange(s, send):
        if len(lay.stages[s]) == 1:
            return moved(send, "col", lay.stages[s][0])
        parts = [
            moved(send[n * lay.cap : (n + 1) * lay.cap], "col", d) for n, d in enumerate(lay.stages[s])
        ]
        return jnp.concatenate(parts, axis=0)

    order = Order(col)
    sends = list(first_stage(lay, targets, col, stored))
    got = [exchange(s, sends[s]) for s in range(FIRST)]
    *rest, pos = rest_stages(lay, targets, col, plans[1, :prods].reshape(-1, stored.shape[-1]), order.gate(stored))
    sends += rest
    got += [exchange(s, sends[s]) for s in stages[FIRST:4]]
    reqs_r, slots_l, slots_r = order.gate(wanted(2 * lay.stored, order.gate(plans[1]), prods))
    asked_r = moved(reqs_r, "row", 1)
    pos_r = moved(pos, "row", -1)
    got += [exchange(s, sends[s]) for s in stages[4:-1]]
    for s in stages[:3]:
        got[s] = order.gate(got[s])
    asked_r = order.gate(asked_r)
    for s in stages[3:-2]:
        got[s] = order.gate(got[s])
    got.append(exchange(stages[-1], order.gate(sends[-1])))
    got[-2] = order.gate(got[-2])
    rows = prods // stored.shape[-1]
    ids = got[lay.self_stage][-1, : 16 * rows : 16].reshape(-1).astype(jnp.int32)
    asked_l = order.gate(asked(2 * lay.stored, order.gate(ids)))
    picked = order.gate(pick(lay, early, RIGHT_PIECES, asked_r, pos, stored, [got[s] for s in early], "pick_right"))
    right = [moved(piece, "row", -1) for piece in picked]
    got[-1] = order.gate(got[-1])
    forwarded = [moved(got[s], "row", -1) for s in late]
    ready = [s for s in stages if s != lay.self_stage]
    picked = pick(lay, ready, LEFT_PIECES, order.gate(asked_l), pos, stored, [got[s] for s in ready], "pick_left")
    left = [moved(piece, "col", -1) for piece in order.gate(picked)]
    right = order.gate(right)
    acc = own_section(lay, order.gate(plans[0]), counts, pos, stored, got)
    out = next_section(
        lay, late, order.token, plans[1], counts, slots_l, slots_r, pos, pos_r, acc, left, sends[lay.self_stage], right, forwarded
    )
    return out[None, None]


def solution(mesh):
    placed = (
        P("row", "col", None, None, None),
        P("row", "col", None),
        P("row", "col", None, None, None),
        P("row", "col", None),
    )
    return jax.shard_map(
        body,
        mesh=mesh,
        in_specs=placed,
        out_specs=P("row", "col", None, None, None),
        check_vma=False,
    )
```

```python
import functools

import jax
import jax.numpy as jnp
from jax import lax
from jax.experimental import pallas as pl
from jax.experimental.pallas import tpu as pltpu
from jax.sharding import PartitionSpec as P

OUTSLOTS = 32
USED = 24
UNROLL = 16
NEXT_UNROLL = 16
FIRST = 1
LEFT_PIECES = 1
RIGHT_PIECES = 1
FIRST_MIB = 62
MIB = 1 << 20

SMEM = pl.BlockSpec(memory_space=pltpu.SMEM)
VMEM = pl.BlockSpec(memory_space=pltpu.VMEM)
HBM = pl.BlockSpec(memory_space=pltpu.HBM)


def cost(us):
    return pl.CostEstimate(flops=0, bytes_accessed=int(us * 3.5e6), transcendentals=0)


def i32(*shape):
    return jax.ShapeDtypeStruct(shape, jnp.int32)


def params(mib):
    return pltpu.CompilerParams(vmem_limit_bytes=mib * MIB)


def moved(value, axis, steps):
    count = lax.axis_size(axis)
    return lax.ppermute(value, axis, [(s, (s + steps) % count) for s in range(count)])


def after(value, *needed):
    return lax.optimization_barrier((value, *needed))[0]


class Order:
    def __init__(self, token):
        self.token = token

    def gate(self, value):
        value, self.token = lax.optimization_barrier((value, self.token))
        return value


class Layout:
    def __init__(self, stored, cols):
        self.stored = stored
        self.cols = cols
        self.cap = (stored + cols - 2) // (cols - 1)
        half = cols // 2
        others = [d for d in range(2, cols) if d != half]
        others.sort(key=lambda d: (half - abs(d - half), d))
        others = others[1:3] + others[:1] + others[3:]
        pieces = min(5, len(others))
        cuts = [len(others) * i // pieces for i in range(pieces + 1)]
        groups = [others[a:b] for a, b in zip(cuts, cuts[1:])]
        self.stages = groups[:3] + [[1]] + groups[3:] + [[half]]
        self.base = [0] * cols
        self.start = []
        at = 0
        for stage in self.stages:
            self.start.append(at)
            for d in stage:
                self.base[d] = at
                at += self.cap
        self.total = at
        self.start.append(at)
        self.self_stage = self.stages.index([1])

    def size(self, s):
        return self.start[s + 1] - self.start[s]


def offset_of(lay, tgt, k, me):
    d = tgt[k] - me
    return jnp.where(d < 0, d + lay.cols, d)


def first_kernel(lay, tgt, col, stored_ref, *rest):
    outs, (buf, found, sem) = rest[:FIRST], rest[FIRST:]
    goals = []
    for n, offset in enumerate(d for stage in lay.stages[:FIRST] for d in stage):
        goal = col[0] + offset
        goals.append(jnp.where(goal >= lay.cols, goal - lay.cols, goal))
    at = [jnp.int32(n * lay.cap) for n in range(len(goals))]
    for k in range(lay.stored):
        target = tgt[k]
        for n, goal in enumerate(goals):
            hit = target == goal
            found[jnp.where(hit, at[n], lay.total)] = k
            at[n] = at[n] + hit.astype(jnp.int32)
    total = lay.start[FIRST]
    for j in range(total):
        pltpu.make_async_copy(stored_ref.at[found[j]], buf.at[j], sem).start()
    pltpu.make_async_copy(buf, buf, sem).wait()
    for s, out in enumerate(outs):
        for j in range(lay.size(s)):
            out[j] = buf[lay.start[s] + j].T


def first_stage(lay, targets, col, stored):
    block = stored.shape[-1]
    return pl.pallas_call(
        functools.partial(first_kernel, lay),
        out_shape=tuple(jax.ShapeDtypeStruct((lay.size(s), block, block), stored.dtype) for s in range(FIRST)),
        in_specs=[SMEM, SMEM, HBM],
        out_specs=(VMEM,) * FIRST,
        scratch_shapes=[
            pltpu.VMEM((lay.start[FIRST], block, block), stored.dtype),
            pltpu.SMEM((lay.total + 1,), jnp.int32),
            pltpu.SemaphoreType.DMA,
        ],
        compiler_params=params(FIRST_MIB),
        name="first_stage",
    )(targets, col, stored)


def rest_kernel(lay, tgt, col, plan, stored_ref, *rest):
    outs, pos, inv, cnt = rest[:-3], rest[-3], rest[-2], rest[-1]
    for d in range(lay.cols):
        cnt[d] = lay.base[d]

    def place(k, carry):
        d = offset_of(lay, tgt, k, col[0])
        q = cnt[d]
        cnt[d] = q + 1
        pos[k] = q
        inv[q] = k
        return carry

    lax.fori_loop(0, lay.stored, place, 0)
    for s in range(FIRST, len(lay.stages)):

        def flip(j, carry, s=s):
            outs[s - FIRST][j] = stored_ref[inv[lay.start[s] + j]].T
            return carry

        lax.fori_loop(0, lay.size(s), flip, 0, unroll=9 if lay.size(s) % 9 == 0 else 1)
    note = outs[lay.self_stage - FIRST]
    block = note.shape[-1]
    for row in range(plan.shape[2] // block):
        line = plan[0, 1:2, row * block : row * block + block].astype(jnp.float32)
        note[lay.size(lay.self_stage), row * 16 : row * 16 + 16, :] = jnp.broadcast_to(line, (16, block)).astype(note.dtype)


def rest_stages(lay, targets, col, plan, stored):
    block = stored.shape[-1]
    shapes = tuple(
        jax.ShapeDtypeStruct((lay.size(s) + (s == lay.self_stage), block, block), stored.dtype)
        for s in range(FIRST, len(lay.stages))
    )
    return pl.pallas_call(
        functools.partial(rest_kernel, lay),
        out_shape=shapes + (i32(lay.stored),),
        in_specs=[SMEM, SMEM, VMEM, VMEM],
        out_specs=(VMEM,) * len(shapes) + (SMEM,),
        scratch_shapes=[pltpu.SMEM((lay.total,), jnp.int32), pltpu.SMEM((lay.cols,), jnp.int32)],
        compiler_params=params(12),
        cost_estimate=cost(0.01),
        name="rest_stages",
    )(targets, col, plan, stored)


def wanted_kernel(prods, plan, reqs_r, slots_l, slots_r, seen_l, seen_r):
    def clear(i, carry):
        seen_l[i] = -1
        seen_r[i] = -1
        return carry

    lax.fori_loop(0, seen_l.shape[0], clear, 0, unroll=6 if seen_l.shape[0] % 6 == 0 else 1)
    for i in range(USED):
        reqs_r[i] = 0

    def step(p, counts):
        sides = ((slots_l, seen_l), (slots_r, seen_r))
        found = [plan[side, 1, p] for side in range(2)]
        known = [seen[which] for (_, seen), which in zip(sides, found)]
        slot = [jnp.where(k < 0, n, k) for k, n in zip(known, counts)]
        for (slots, seen), which, at in zip(sides, found, slot):
            seen[which] = at
            slots[p] = at
        reqs_r[slot[1]] = found[1]
        return tuple(n + (k < 0).astype(jnp.int32) for k, n in zip(known, counts))

    lax.fori_loop(0, prods, step, (jnp.int32(0), jnp.int32(0)), unroll=4)


def wanted(panel_size, plan, prods):
    return pl.pallas_call(
        functools.partial(wanted_kernel, prods),
        out_shape=(i32(USED), i32(prods), i32(prods)),
        in_specs=[SMEM],
        out_specs=(SMEM,) * 3,
        scratch_shapes=[pltpu.SMEM((panel_size,), jnp.int32)] * 2,
        cost_estimate=cost(0.01),
        name="wanted",
    )(plan)


def asked_kernel(ids, reqs, seen):
    def clear(i, carry):
        seen[i] = 0
        return carry

    lax.fori_loop(0, seen.shape[0], clear, 0, unroll=6 if seen.shape[0] % 6 == 0 else 1)

    def step(p, n):
        which = ids[p]
        known = seen[which]
        reqs[n] = which
        seen[which] = 1
        return n + 1 - known

    lax.fori_loop(0, ids.shape[0], step, jnp.int32(0), unroll=4)


def asked(panel_size, ids):
    return pl.pallas_call(
        asked_kernel,
        out_shape=i32(USED + 1),
        in_specs=[SMEM],
        out_specs=SMEM,
        scratch_shapes=[pltpu.SMEM((panel_size,), jnp.int32)],
        name="asked",
    )(ids)


def pick_kernel(lay, stages, pieces, req, pos, stored_ref, *rest):
    parts, outs = rest[: len(stages)], rest[len(stages) :]
    size = USED // pieces
    for piece, out in enumerate(outs):
        for n in range(size):
            which = req[piece * size + n]
            lower = which >= lay.stored
            q = pos[jnp.where(lower, which - lay.stored, 0)]
            value = stored_ref[jnp.where(lower, 0, which)]
            for s, part in zip(stages, parts):
                at = jnp.clip(q - lay.start[s], 0, lay.size(s) - 1)
                value = jnp.where(lower & (q >= lay.start[s]), part[at], value)
            out[n] = value


def pick(lay, stages, pieces, req, pos, stored, parts, name):
    block = stored.shape[-1]
    return pl.pallas_call(
        functools.partial(pick_kernel, lay, stages, pieces),
        out_shape=(jax.ShapeDtypeStruct((USED // pieces, block, block), stored.dtype),) * pieces,
        in_specs=[SMEM, SMEM, VMEM] + [VMEM] * len(parts),
        out_specs=(VMEM,) * pieces,
        compiler_params=params(16),
        name=name,
    )(req, pos, stored, *parts)


def multiply(count, entry, left, right, acc):
    spare = acc.shape[0] - 1

    def group(g, carry):
        found = []
        for u in range(UNROLL):
            p = g * UNROLL + u
            i, j, o = entry(p)
            o = jnp.where(p < count, o, spare)
            found.append((o, jnp.dot(left[i], right[j], preferred_element_type=jnp.float32)))
        for o, term in found:
            acc[o] += term
        return carry

    lax.fori_loop(0, (count + UNROLL - 1) // UNROLL, group, 0)


def own_kernel(lay, prods, plan, counts, pos, stored_ref, *rest):
    parts = rest[: len(lay.stages)]
    acc, panel, sem = rest[len(lay.stages) :]
    copies = [pltpu.make_async_copy(stored_ref, panel.at[pl.ds(0, lay.stored)], sem.at[0])]
    for s, part in enumerate(parts):
        copies.append(
            pltpu.make_async_copy(
                part.at[pl.ds(0, lay.size(s))], panel.at[pl.ds(lay.stored + lay.start[s], lay.size(s))], sem.at[s + 1]
            )
        )
    for copy in copies:
        copy.start()

    def zero(o, carry):
        acc[o] = jnp.zeros(acc.shape[1:], acc.dtype)
        return carry

    lax.fori_loop(0, acc.shape[0], zero, 0)
    for copy in copies:
        copy.wait()

    def where(which):
        lower = which >= lay.stored
        return jnp.where(lower, lay.stored + pos[jnp.where(lower, which - lay.stored, 0)], which)

    def entry(p):
        return where(plan[0, 0, p]), where(plan[1, 0, p]), plan[2, 0, p]

    multiply(counts[0], entry, panel, panel, acc)


def own_section(lay, plan, counts, pos, stored, parts):
    block = stored.shape[-1]
    prods = plan.shape[2]
    return pl.pallas_call(
        functools.partial(own_kernel, lay, prods),
        out_shape=jax.ShapeDtypeStruct((OUTSLOTS + 1, block, block), jnp.float32),
        in_specs=[SMEM, SMEM, SMEM, VMEM] + [VMEM] * len(parts),
        out_specs=VMEM,
        scratch_shapes=[
            pltpu.VMEM((lay.stored + lay.total, block, block), stored.dtype),
            pltpu.SemaphoreType.DMA((len(parts) + 1,)),
        ],
        compiler_params=params(20),
        cost_estimate=cost(0.01),
        name="own_section",
    )(plan, counts, pos, stored, *parts)


def places_kernel(lay, late, plan, counts, slots_l, slots_r, pos, pos_r, out):
    own_from, own_to = lay.start[lay.self_stage], lay.start[lay.self_stage + 1]
    late_from = lay.start[late[0]]

    def step(p, carry):
        left_id, right_id = plan[0, 1, p], plan[1, 1, p]
        lower = left_id >= lay.stored
        q = pos[jnp.where(lower, left_id - lay.stored, 0)]
        out[0, p] = jnp.where(lower & (q >= own_from) & (q < own_to), USED + q - own_from, slots_l[p])
        lower = right_id >= lay.stored
        q = pos_r[jnp.where(lower, right_id - lay.stored, 0)]
        out[1, p] = jnp.where(lower & (q >= late_from), USED + q - late_from, slots_r[p])
        out[2, p] = jnp.where(p < counts[1], plan[2, 1, p], OUTSLOTS)
        return carry

    lax.fori_loop(0, plan.shape[2], step, 0, unroll=4)


def places(lay, late, plan, counts, slots_l, slots_r, pos, pos_r):
    return pl.pallas_call(
        functools.partial(places_kernel, lay, late),
        out_shape=i32(3, plan.shape[2]),
        in_specs=[SMEM] * 6,
        out_specs=SMEM,
        name="places",
    )(plan, counts, slots_l, slots_r, pos, pos_r)


def either(n, first, first_size, others):
    value = first[jnp.minimum(n, first_size - 1)]
    at = first_size
    for part, size in others:
        value = jnp.where(n >= at, part[jnp.clip(n - at, 0, size - 1)], value)
        at += size
    return value


def next_kernel(lay, late, token, spots, counts, old, self_ref, left, right, *rest):
    parts, (acc, out) = rest[:-2], rest[-2:]
    lefts = [(self_ref, lay.size(lay.self_stage))]
    rights = [(part, lay.size(s)) for s, part in zip(late, parts)]

    def group(g, carry):
        found = []
        for u in range(NEXT_UNROLL):
            p = g * NEXT_UNROLL + u
            i, j, o = spots[0, p], spots[1, p], spots[2, p]
            a = either(i, left, USED, lefts)
            b = either(j, right, USED, rights)
            found.append((o, jnp.dot(a, b, preferred_element_type=jnp.float32)))
        for o, term in found:
            acc[o] += term
        return carry

    lax.fori_loop(0, (counts[1] + NEXT_UNROLL - 1) // NEXT_UNROLL, group, 0)
    for o in range(OUTSLOTS):
        out[o] = acc[o].astype(out.dtype)


def next_section(lay, late, token, spots, counts, acc, self_part, left, right, parts):
    block = self_part.shape[-1]
    return pl.pallas_call(
        functools.partial(next_kernel, lay, late),
        out_shape=(
            jax.ShapeDtypeStruct(acc.shape, acc.dtype),
            jax.ShapeDtypeStruct((OUTSLOTS, block, block), self_part.dtype),
        ),
        in_specs=[SMEM] * 3 + [VMEM] * (4 + len(parts)),
        out_specs=(VMEM, VMEM),
        input_output_aliases={3: 0},
        compiler_params=params(20),
        cost_estimate=cost(0.01),
        name="next_section",
    )(token, spots, counts, acc, self_part, left, right, *parts)[1]


FLIGHT = 2
EARLY = 6


def body(upper_blocks, block_targets, product_plan, live_counts):
    stored = upper_blocks[0, 0]
    targets = block_targets[0, 0]
    counts = live_counts[0, 0]
    plan = jnp.transpose(product_plan[0, 0], (2, 0, 1))
    prods = plan.shape[2]
    lay = Layout(stored.shape[0], lax.axis_size("col"))
    stages = list(range(len(lay.stages)))
    early, late = stages[:EARLY], stages[EARLY:]
    col = lax.axis_index("col").astype(jnp.int32).reshape(1)

    def exchange(s, send):
        if len(lay.stages[s]) == 1:
            return moved(send, "col", lay.stages[s][0])
        parts = [
            moved(send[n * lay.cap : (n + 1) * lay.cap], "col", d) for n, d in enumerate(lay.stages[s])
        ]
        return jnp.concatenate(parts, axis=0)

    order = Order(col)
    sends = list(order.gate(first_stage(lay, targets, col, stored)))
    got = [exchange(s, sends[s]) for s in range(FIRST)]
    *rest, pos = rest_stages(lay, targets, col, plan, order.gate(stored))
    sends += rest
    got += [exchange(s, sends[s]) for s in stages[FIRST:-1]]
    for s in stages[:2]:
        got[s] = order.gate(got[s])
    reqs_r, slots_l, slots_r = order.gate(wanted(2 * lay.stored, order.gate(plan), prods))
    asked_r = moved(reqs_r, "row", 1)
    pos_r = moved(pos, "row", -1)
    got[2] = order.gate(got[2])
    got[3] = order.gate(got[3])
    asked_r, pos_r = order.gate((asked_r, pos_r))
    rows = prods // stored.shape[-1]
    ids = got[lay.self_stage][-1, : 16 * rows : 16].reshape(-1).astype(jnp.int32)
    asked_l = order.gate(asked(2 * lay.stored, order.gate(ids)))
    spots = order.gate(places(lay, late, plan, counts, slots_l, slots_r, pos, pos_r))
    for s in stages[4:-1]:
        got[s] = order.gate(got[s])
    got.append(exchange(stages[-1], order.gate(sends[-1])))
    picked = order.gate(pick(lay, early, RIGHT_PIECES, asked_r, pos, stored, [got[s] for s in early], "pick_right"))
    right = [moved(piece, "row", -1) for piece in picked]
    got[-1] = order.gate(got[-1])
    forwarded = [moved(got[s], "row", -1) for s in late]
    ready = [s for s in stages if s != lay.self_stage]
    picked = pick(lay, ready, LEFT_PIECES, order.gate(asked_l), pos, stored, [got[s] for s in ready], "pick_left")
    left = [moved(piece, "col", -1) for piece in order.gate(picked)]
    acc = own_section(lay, plan, counts, pos, stored, got)
    out = next_section(lay, late, order.token, spots, counts, acc, sends[lay.self_stage], *left, *right, forwarded)
    return out[None, None]


def solution(mesh):
    placed = (
        P("row", "col", None, None, None),
        P("row", "col", None),
        P("row", "col", None, None, None),
        P("row", "col", None),
    )
    return jax.shard_map(
        body,
        mesh=mesh,
        in_specs=placed,
        out_specs=P("row", "col", None, None, None),
        check_vma=False,
    )
```

```python
import functools

import jax
import jax.numpy as jnp
from jax import lax
from jax.experimental import pallas as pl
from jax.experimental.pallas import tpu as pltpu
from jax.sharding import PartitionSpec as P

OUTSLOTS = 32
USED = 24
UNROLL = 16
NEXT_UNROLL = 16
FIRST = 1
LEFT_PIECES = 1
RIGHT_PIECES = 1
FIRST_MIB = 62
MIB = 1 << 20

SMEM = pl.BlockSpec(memory_space=pltpu.SMEM)
VMEM = pl.BlockSpec(memory_space=pltpu.VMEM)
HBM = pl.BlockSpec(memory_space=pltpu.HBM)


def cost(us):
    return pl.CostEstimate(flops=0, bytes_accessed=int(us * 3.5e6), transcendentals=0)


def i32(*shape):
    return jax.ShapeDtypeStruct(shape, jnp.int32)


def params(mib):
    return pltpu.CompilerParams(vmem_limit_bytes=mib * MIB)


def moved(value, axis, steps):
    count = lax.axis_size(axis)
    return lax.ppermute(value, axis, [(s, (s + steps) % count) for s in range(count)])


def after(value, *needed):
    return lax.optimization_barrier((value, *needed))[0]


class Order:
    def __init__(self, token):
        self.token = token

    def gate(self, value):
        value, self.token = lax.optimization_barrier((value, self.token))
        return value


class Layout:
    def __init__(self, stored, cols):
        self.stored = stored
        self.cols = cols
        self.cap = (stored + cols - 2) // (cols - 1)
        half = cols // 2
        others = [d for d in range(2, cols) if d != half]
        others.sort(key=lambda d: (half - abs(d - half), d))
        others = others[1:2] + others[:1] + others[2:3] + others[3:]
        pieces = min(5, len(others))
        cuts = [len(others) * i // pieces for i in range(pieces + 1)]
        groups = [others[a:b] for a, b in zip(cuts, cuts[1:])]
        self.stages = groups[:3] + [[1]] + groups[3:] + [[half]]
        self.base = [0] * cols
        self.start = []
        at = 0
        for stage in self.stages:
            self.start.append(at)
            for d in stage:
                self.base[d] = at
                at += self.cap
        self.total = at
        self.start.append(at)
        self.self_stage = self.stages.index([1])

    def size(self, s):
        return self.start[s + 1] - self.start[s]


def offset_of(lay, tgt, k, me):
    d = tgt[k] - me
    return jnp.where(d < 0, d + lay.cols, d)


def first_kernel(lay, tgt, col, stored_ref, *rest):
    outs, (buf, found, sem) = rest[:FIRST], rest[FIRST:]
    goals = []
    for n, offset in enumerate(d for stage in lay.stages[:FIRST] for d in stage):
        goal = col[0] + offset
        goals.append(jnp.where(goal >= lay.cols, goal - lay.cols, goal))
    at = [jnp.int32(n * lay.cap) for n in range(len(goals))]
    for k in range(lay.stored):
        target = tgt[k]
        for n, goal in enumerate(goals):
            hit = target == goal
            found[jnp.where(hit, at[n], lay.total)] = k
            at[n] = at[n] + hit.astype(jnp.int32)
    total = lay.start[FIRST]
    for j in range(total):
        pltpu.make_async_copy(stored_ref.at[found[j]], buf.at[j], sem).start()
    pltpu.make_async_copy(buf, buf, sem).wait()
    for s, out in enumerate(outs):
        for j in range(lay.size(s)):
            out[j] = buf[lay.start[s] + j].T


def first_stage(lay, targets, col, stored):
    block = stored.shape[-1]
    return pl.pallas_call(
        functools.partial(first_kernel, lay),
        out_shape=tuple(jax.ShapeDtypeStruct((lay.size(s), block, block), stored.dtype) for s in range(FIRST)),
        in_specs=[SMEM, SMEM, HBM],
        out_specs=(VMEM,) * FIRST,
        scratch_shapes=[
            pltpu.VMEM((lay.start[FIRST], block, block), stored.dtype),
            pltpu.SMEM((lay.total + 1,), jnp.int32),
            pltpu.SemaphoreType.DMA,
        ],
        compiler_params=params(FIRST_MIB),
        name="first_stage",
    )(targets, col, stored)


def rest_kernel(lay, tgt, col, plan, stored_ref, *rest):
    outs, pos, inv, cnt = rest[:-3], rest[-3], rest[-2], rest[-1]
    for d in range(lay.cols):
        cnt[d] = lay.base[d]

    def place(k, carry):
        d = offset_of(lay, tgt, k, col[0])
        q = cnt[d]
        cnt[d] = q + 1
        pos[k] = q
        inv[q] = k
        return carry

    lax.fori_loop(0, lay.stored, place, 0)
    for s in range(FIRST, len(lay.stages)):

        def flip(j, carry, s=s):
            outs[s - FIRST][j] = stored_ref[inv[lay.start[s] + j]].T
            return carry

        lax.fori_loop(0, lay.size(s), flip, 0, unroll=9 if lay.size(s) % 9 == 0 else 1)
    note = outs[lay.self_stage - FIRST]
    block = note.shape[-1]
    for row in range(plan.shape[2] // block):
        line = plan[0, 1:2, row * block : row * block + block].astype(jnp.float32)
        note[lay.size(lay.self_stage), row * 16 : row * 16 + 16, :] = jnp.broadcast_to(line, (16, block)).astype(note.dtype)


def rest_stages(lay, targets, col, plan, stored):
    block = stored.shape[-1]
    shapes = tuple(
        jax.ShapeDtypeStruct((lay.size(s) + (s == lay.self_stage), block, block), stored.dtype)
        for s in range(FIRST, len(lay.stages))
    )
    return pl.pallas_call(
        functools.partial(rest_kernel, lay),
        out_shape=shapes + (i32(lay.stored),),
        in_specs=[SMEM, SMEM, VMEM, VMEM],
        out_specs=(VMEM,) * len(shapes) + (SMEM,),
        scratch_shapes=[pltpu.SMEM((lay.total,), jnp.int32), pltpu.SMEM((lay.cols,), jnp.int32)],
        compiler_params=params(12),
        cost_estimate=cost(0.01),
        name="rest_stages",
    )(targets, col, plan, stored)


def wanted_kernel(prods, plan, reqs_r, slots_l, slots_r, seen_l, seen_r):
    def clear(i, carry):
        seen_l[i] = -1
        seen_r[i] = -1
        return carry

    lax.fori_loop(0, seen_l.shape[0], clear, 0, unroll=6 if seen_l.shape[0] % 6 == 0 else 1)
    for i in range(USED):
        reqs_r[i] = 0

    def step(p, counts):
        sides = ((slots_l, seen_l), (slots_r, seen_r))
        found = [plan[side, 1, p] for side in range(2)]
        known = [seen[which] for (_, seen), which in zip(sides, found)]
        slot = [jnp.where(k < 0, n, k) for k, n in zip(known, counts)]
        for (slots, seen), which, at in zip(sides, found, slot):
            seen[which] = at
            slots[p] = at
        reqs_r[slot[1]] = found[1]
        return tuple(n + (k < 0).astype(jnp.int32) for k, n in zip(known, counts))

    lax.fori_loop(0, prods, step, (jnp.int32(0), jnp.int32(0)), unroll=4)


def wanted(panel_size, plan, prods):
    return pl.pallas_call(
        functools.partial(wanted_kernel, prods),
        out_shape=(i32(USED), i32(prods), i32(prods)),
        in_specs=[SMEM],
        out_specs=(SMEM,) * 3,
        scratch_shapes=[pltpu.SMEM((panel_size,), jnp.int32)] * 2,
        cost_estimate=cost(0.01),
        name="wanted",
    )(plan)


def asked_kernel(ids, reqs, seen):
    def clear(i, carry):
        seen[i] = 0
        return carry

    lax.fori_loop(0, seen.shape[0], clear, 0, unroll=6 if seen.shape[0] % 6 == 0 else 1)

    def step(p, n):
        which = ids[p]
        known = seen[which]
        reqs[n] = which
        seen[which] = 1
        return n + 1 - known

    lax.fori_loop(0, ids.shape[0], step, jnp.int32(0), unroll=4)


def asked(panel_size, ids):
    return pl.pallas_call(
        asked_kernel,
        out_shape=i32(USED + 1),
        in_specs=[SMEM],
        out_specs=SMEM,
        scratch_shapes=[pltpu.SMEM((panel_size,), jnp.int32)],
        name="asked",
    )(ids)


def pick_kernel(lay, stages, pieces, req, pos, stored_ref, *rest):
    parts, outs = rest[: len(stages)], rest[len(stages) :]
    size = USED // pieces
    for piece, out in enumerate(outs):
        for n in range(size):
            which = req[piece * size + n]
            lower = which >= lay.stored
            q = pos[jnp.where(lower, which - lay.stored, 0)]
            value = stored_ref[jnp.where(lower, 0, which)]
            for s, part in zip(stages, parts):
                at = jnp.clip(q - lay.start[s], 0, lay.size(s) - 1)
                value = jnp.where(lower & (q >= lay.start[s]), part[at], value)
            out[n] = value


def pick(lay, stages, pieces, req, pos, stored, parts, name):
    block = stored.shape[-1]
    return pl.pallas_call(
        functools.partial(pick_kernel, lay, stages, pieces),
        out_shape=(jax.ShapeDtypeStruct((USED // pieces, block, block), stored.dtype),) * pieces,
        in_specs=[SMEM, SMEM, VMEM] + [VMEM] * len(parts),
        out_specs=(VMEM,) * pieces,
        compiler_params=params(16),
        name=name,
    )(req, pos, stored, *parts)


def multiply(count, entry, left, right, acc):
    spare = acc.shape[0] - 1

    def group(g, carry):
        found = []
        for u in range(UNROLL):
            p = g * UNROLL + u
            i, j, o = entry(p)
            o = jnp.where(p < count, o, spare)
            found.append((o, jnp.dot(left[i], right[j], preferred_element_type=jnp.float32)))
        for o, term in found:
            acc[o] += term
        return carry

    lax.fori_loop(0, (count + UNROLL - 1) // UNROLL, group, 0)


def own_kernel(lay, prods, plan, counts, pos, stored_ref, *rest):
    parts = rest[: len(lay.stages)]
    acc, panel, sem = rest[len(lay.stages) :]
    copies = [pltpu.make_async_copy(stored_ref, panel.at[pl.ds(0, lay.stored)], sem.at[0])]
    for s, part in enumerate(parts):
        copies.append(
            pltpu.make_async_copy(
                part.at[pl.ds(0, lay.size(s))], panel.at[pl.ds(lay.stored + lay.start[s], lay.size(s))], sem.at[s + 1]
            )
        )
    for copy in copies:
        copy.start()

    def zero(o, carry):
        acc[o] = jnp.zeros(acc.shape[1:], acc.dtype)
        return carry

    lax.fori_loop(0, acc.shape[0], zero, 0)
    for copy in copies:
        copy.wait()

    def where(which):
        lower = which >= lay.stored
        return jnp.where(lower, lay.stored + pos[jnp.where(lower, which - lay.stored, 0)], which)

    def entry(p):
        return where(plan[0, 0, p]), where(plan[1, 0, p]), plan[2, 0, p]

    multiply(counts[0], entry, panel, panel, acc)


def own_section(lay, plan, counts, pos, stored, parts):
    block = stored.shape[-1]
    prods = plan.shape[2]
    return pl.pallas_call(
        functools.partial(own_kernel, lay, prods),
        out_shape=jax.ShapeDtypeStruct((OUTSLOTS + 1, block, block), jnp.float32),
        in_specs=[SMEM, SMEM, SMEM, VMEM] + [VMEM] * len(parts),
        out_specs=VMEM,
        scratch_shapes=[
            pltpu.VMEM((lay.stored + lay.total, block, block), stored.dtype),
            pltpu.SemaphoreType.DMA((len(parts) + 1,)),
        ],
        compiler_params=params(20),
        cost_estimate=cost(0.01),
        name="own_section",
    )(plan, counts, pos, stored, *parts)


def places_kernel(lay, late, plan, counts, slots_l, slots_r, pos, pos_r, out):
    own_from, own_to = lay.start[lay.self_stage], lay.start[lay.self_stage + 1]
    late_from = lay.start[late[0]]

    def step(p, carry):
        left_id, right_id = plan[0, 1, p], plan[1, 1, p]
        lower = left_id >= lay.stored
        q = pos[jnp.where(lower, left_id - lay.stored, 0)]
        out[0, p] = jnp.where(lower & (q >= own_from) & (q < own_to), USED + q - own_from, slots_l[p])
        lower = right_id >= lay.stored
        q = pos_r[jnp.where(lower, right_id - lay.stored, 0)]
        out[1, p] = jnp.where(lower & (q >= late_from), USED + q - late_from, slots_r[p])
        out[2, p] = jnp.where(p < counts[1], plan[2, 1, p], OUTSLOTS)
        return carry

    lax.fori_loop(0, plan.shape[2], step, 0, unroll=4)


def places(lay, late, plan, counts, slots_l, slots_r, pos, pos_r):
    return pl.pallas_call(
        functools.partial(places_kernel, lay, late),
        out_shape=i32(3, plan.shape[2]),
        in_specs=[SMEM] * 6,
        out_specs=SMEM,
        name="places",
    )(plan, counts, slots_l, slots_r, pos, pos_r)


def either(n, first, first_size, others):
    value = first[jnp.minimum(n, first_size - 1)]
    at = first_size
    for part, size in others:
        value = jnp.where(n >= at, part[jnp.clip(n - at, 0, size - 1)], value)
        at += size
    return value


def next_kernel(lay, late, token, spots, counts, old, self_ref, left, right, *rest):
    parts, (acc, out) = rest[:-2], rest[-2:]
    lefts = [(self_ref, lay.size(lay.self_stage))]
    rights = [(part, lay.size(s)) for s, part in zip(late, parts)]

    def group(g, carry):
        found = []
        for u in range(NEXT_UNROLL):
            p = g * NEXT_UNROLL + u
            i, j, o = spots[0, p], spots[1, p], spots[2, p]
            a = either(i, left, USED, lefts)
            b = either(j, right, USED, rights)
            found.append((o, jnp.dot(a, b, preferred_element_type=jnp.float32)))
        for o, term in found:
            acc[o] += term
        return carry

    lax.fori_loop(0, (counts[1] + NEXT_UNROLL - 1) // NEXT_UNROLL, group, 0)
    for o in range(OUTSLOTS):
        out[o] = acc[o].astype(out.dtype)


def next_section(lay, late, token, spots, counts, acc, self_part, left, right, parts):
    block = self_part.shape[-1]
    return pl.pallas_call(
        functools.partial(next_kernel, lay, late),
        out_shape=(
            jax.ShapeDtypeStruct(acc.shape, acc.dtype),
            jax.ShapeDtypeStruct((OUTSLOTS, block, block), self_part.dtype),
        ),
        in_specs=[SMEM] * 3 + [VMEM] * (4 + len(parts)),
        out_specs=(VMEM, VMEM),
        input_output_aliases={3: 0},
        compiler_params=params(20),
        cost_estimate=cost(0.01),
        name="next_section",
    )(token, spots, counts, acc, self_part, left, right, *parts)[1]


FLIGHT = 2
EARLY = 6


def body(upper_blocks, block_targets, product_plan, live_counts):
    stored = upper_blocks[0, 0]
    targets = block_targets[0, 0]
    counts = live_counts[0, 0]
    plan = jnp.transpose(product_plan[0, 0], (2, 0, 1))
    prods = plan.shape[2]
    lay = Layout(stored.shape[0], lax.axis_size("col"))
    stages = list(range(len(lay.stages)))
    early, late = stages[:EARLY], stages[EARLY:]
    col = lax.axis_index("col").astype(jnp.int32).reshape(1)

    def exchange(s, send):
        if len(lay.stages[s]) == 1:
            return moved(send, "col", lay.stages[s][0])
        parts = [
            moved(send[n * lay.cap : (n + 1) * lay.cap], "col", d) for n, d in enumerate(lay.stages[s])
        ]
        return jnp.concatenate(parts, axis=0)

    order = Order(col)
    sends = list(order.gate(first_stage(lay, targets, col, stored)))
    got = [exchange(s, sends[s]) for s in range(FIRST)]
    *rest, pos = rest_stages(lay, targets, col, plan, order.gate(stored))
    sends += rest
    got += [exchange(s, sends[s]) for s in stages[FIRST:-1]]
    for s in stages[:2]:
        got[s] = order.gate(got[s])
    reqs_r, slots_l, slots_r = order.gate(wanted(2 * lay.stored, order.gate(plan), prods))
    asked_r = moved(reqs_r, "row", 1)
    pos_r = moved(pos, "row", -1)
    got[2] = order.gate(got[2])
    got[3] = order.gate(got[3])
    asked_r, pos_r = order.gate((asked_r, pos_r))
    rows = prods // stored.shape[-1]
    ids = got[lay.self_stage][-1, : 16 * rows : 16].reshape(-1).astype(jnp.int32)
    asked_l = order.gate(asked(2 * lay.stored, order.gate(ids)))
    spots = order.gate(places(lay, late, plan, counts, slots_l, slots_r, pos, pos_r))
    for s in stages[4:-1]:
        got[s] = order.gate(got[s])
    got.append(exchange(stages[-1], order.gate(sends[-1])))
    picked = order.gate(pick(lay, early, RIGHT_PIECES, asked_r, pos, stored, [got[s] for s in early], "pick_right"))
    right = [moved(piece, "row", -1) for piece in picked]
    got[-1] = order.gate(got[-1])
    forwarded = [moved(got[s], "row", -1) for s in late]
    ready = [s for s in stages if s != lay.self_stage]
    picked = pick(lay, ready, LEFT_PIECES, order.gate(asked_l), pos, stored, [got[s] for s in ready], "pick_left")
    left = [moved(piece, "col", -1) for piece in order.gate(picked)]
    acc = own_section(lay, plan, counts, pos, stored, got)
    out = next_section(lay, late, order.token, spots, counts, acc, sends[lay.self_stage], *left, *right, forwarded)
    return out[None, None]


def solution(mesh):
    placed = (
        P("row", "col", None, None, None),
        P("row", "col", None),
        P("row", "col", None, None, None),
        P("row", "col", None),
    )
    return jax.shard_map(
        body,
        mesh=mesh,
        in_specs=placed,
        out_specs=P("row", "col", None, None, None),
        check_vma=False,
    )
```

```python
import functools

import jax
import jax.numpy as jnp
from jax import lax
from jax.experimental import pallas as pl
from jax.experimental.pallas import tpu as pltpu
from jax.sharding import PartitionSpec as P

OUTSLOTS = 32
USED = 24
UNROLL = 16
NEXT_UNROLL = 32
FIRST = 1
LEFT_PIECES = 1
RIGHT_PIECES = 1
FIRST_MIB = 61
MIB = 1 << 20

SMEM = pl.BlockSpec(memory_space=pltpu.SMEM)
VMEM = pl.BlockSpec(memory_space=pltpu.VMEM)
HBM = pl.BlockSpec(memory_space=pltpu.HBM)


def cost(us):
    return pl.CostEstimate(flops=0, bytes_accessed=int(us * 3.5e6), transcendentals=0)


def i32(*shape):
    return jax.ShapeDtypeStruct(shape, jnp.int32)


def params(mib):
    return pltpu.CompilerParams(vmem_limit_bytes=mib * MIB)


def moved(value, axis, steps):
    count = lax.axis_size(axis)
    return lax.ppermute(value, axis, [(s, (s + steps) % count) for s in range(count)])


def after(value, *needed):
    return lax.optimization_barrier((value, *needed))[0]


class Order:
    def __init__(self, token):
        self.token = token

    def gate(self, value):
        value, self.token = lax.optimization_barrier((value, self.token))
        return value


class Layout:
    def __init__(self, stored, cols):
        self.stored = stored
        self.cols = cols
        self.cap = (stored + cols - 2) // (cols - 1)
        half = cols // 2
        others = [d for d in range(2, cols) if d != half]
        others.sort(key=lambda d: (half - abs(d - half), d))
        others = others[1:2] + others[:1] + others[2:3] + others[3:]
        pieces = min(5, len(others))
        cuts = [len(others) * i // pieces for i in range(pieces + 1)]
        groups = [others[a:b] for a, b in zip(cuts, cuts[1:])]
        self.stages = groups[:3] + [[1]] + groups[3:] + [[half]]
        self.base = [0] * cols
        self.start = []
        at = 0
        for stage in self.stages:
            self.start.append(at)
            for d in stage:
                self.base[d] = at
                at += self.cap
        self.total = at
        self.start.append(at)
        self.self_stage = self.stages.index([1])

    def size(self, s):
        return self.start[s + 1] - self.start[s]


def offset_of(lay, tgt, k, me):
    d = tgt[k] - me
    return jnp.where(d < 0, d + lay.cols, d)


def first_kernel(lay, tgt, col, stored_ref, *rest):
    outs, (buf, found, sem) = rest[:FIRST], rest[FIRST:]
    goals = []
    for n, offset in enumerate(d for stage in lay.stages[:FIRST] for d in stage):
        goal = col[0] + offset
        goals.append(jnp.where(goal >= lay.cols, goal - lay.cols, goal))
    at = [jnp.int32(n * lay.cap) for n in range(len(goals))]
    for k in range(lay.stored):
        target = tgt[k]
        for n, goal in enumerate(goals):
            hit = target == goal
            found[jnp.where(hit, at[n], lay.total)] = k
            at[n] = at[n] + hit.astype(jnp.int32)
    total = lay.start[FIRST]
    for j in range(total):
        pltpu.make_async_copy(stored_ref.at[found[j]], buf.at[j], sem).start()
    pltpu.make_async_copy(buf, buf, sem).wait()
    for s, out in enumerate(outs):
        for j in range(lay.size(s)):
            out[j] = buf[lay.start[s] + j].T


def first_stage(lay, targets, col, stored):
    block = stored.shape[-1]
    return pl.pallas_call(
        functools.partial(first_kernel, lay),
        out_shape=tuple(jax.ShapeDtypeStruct((lay.size(s), block, block), stored.dtype) for s in range(FIRST)),
        in_specs=[SMEM, SMEM, HBM],
        out_specs=(VMEM,) * FIRST,
        scratch_shapes=[
            pltpu.VMEM((lay.start[FIRST], block, block), stored.dtype),
            pltpu.SMEM((lay.total + 1,), jnp.int32),
            pltpu.SemaphoreType.DMA,
        ],
        compiler_params=params(FIRST_MIB),
        name="first_stage",
    )(targets, col, stored)


def rest_kernel(lay, tgt, col, plan, stored_ref, *rest):
    outs, pos, inv, cnt = rest[:-3], rest[-3], rest[-2], rest[-1]
    for d in range(lay.cols):
        cnt[d] = lay.base[d]

    def place(k, carry):
        d = offset_of(lay, tgt, k, col[0])
        q = cnt[d]
        cnt[d] = q + 1
        pos[k] = q
        inv[q] = k
        return carry

    lax.fori_loop(0, lay.stored, place, 0)
    for s in range(FIRST, len(lay.stages)):

        def flip(j, carry, s=s):
            outs[s - FIRST][j] = stored_ref[inv[lay.start[s] + j]].T
            return carry

        lax.fori_loop(0, lay.size(s), flip, 0, unroll=9 if lay.size(s) % 9 == 0 else 1)
    note = outs[lay.self_stage - FIRST]
    block = note.shape[-1]
    for row in range(plan.shape[2] // block):
        line = plan[0, 1:2, row * block : row * block + block].astype(jnp.float32)
        note[lay.size(lay.self_stage), row * 16 : row * 16 + 16, :] = jnp.broadcast_to(line, (16, block)).astype(note.dtype)


def rest_stages(lay, targets, col, plan, stored):
    block = stored.shape[-1]
    shapes = tuple(
        jax.ShapeDtypeStruct((lay.size(s) + (s == lay.self_stage), block, block), stored.dtype)
        for s in range(FIRST, len(lay.stages))
    )
    return pl.pallas_call(
        functools.partial(rest_kernel, lay),
        out_shape=shapes + (i32(lay.stored),),
        in_specs=[SMEM, SMEM, VMEM, VMEM],
        out_specs=(VMEM,) * len(shapes) + (SMEM,),
        scratch_shapes=[pltpu.SMEM((lay.total,), jnp.int32), pltpu.SMEM((lay.cols,), jnp.int32)],
        compiler_params=params(12),
        cost_estimate=cost(0.01),
        name="rest_stages",
    )(targets, col, plan, stored)


def wanted_kernel(prods, plan, reqs_r, slots_l, slots_r, seen_l, seen_r):
    def clear(i, carry):
        seen_l[i] = -1
        seen_r[i] = -1
        return carry

    lax.fori_loop(0, seen_l.shape[0], clear, 0, unroll=6 if seen_l.shape[0] % 6 == 0 else 1)
    for i in range(USED):
        reqs_r[i] = 0

    def step(p, counts):
        sides = ((slots_l, seen_l), (slots_r, seen_r))
        found = [plan[side, 1, p] for side in range(2)]
        known = [seen[which] for (_, seen), which in zip(sides, found)]
        slot = [jnp.where(k < 0, n, k) for k, n in zip(known, counts)]
        for (slots, seen), which, at in zip(sides, found, slot):
            seen[which] = at
            slots[p] = at
        reqs_r[slot[1]] = found[1]
        return tuple(n + (k < 0).astype(jnp.int32) for k, n in zip(known, counts))

    lax.fori_loop(0, prods, step, (jnp.int32(0), jnp.int32(0)), unroll=4)


def wanted(panel_size, plan, prods):
    return pl.pallas_call(
        functools.partial(wanted_kernel, prods),
        out_shape=(i32(USED), i32(prods), i32(prods)),
        in_specs=[SMEM],
        out_specs=(SMEM,) * 3,
        scratch_shapes=[pltpu.SMEM((panel_size,), jnp.int32)] * 2,
        cost_estimate=cost(0.01),
        name="wanted",
    )(plan)


def panel_place(lay, pos, which):
    lower = which >= lay.stored
    return jnp.where(lower, lay.stored + pos[jnp.where(lower, which - lay.stored, 0)], which)


def asked_kernel(lay, ids, pos, spots, seen):
    def clear(i, carry):
        seen[i] = 0
        return carry

    lax.fori_loop(0, seen.shape[0], clear, 0, unroll=6 if seen.shape[0] % 6 == 0 else 1)

    def step(p, n):
        which = ids[p]
        known = seen[which]
        spots[n] = panel_place(lay, pos, which)
        seen[which] = 1
        return n + 1 - known

    lax.fori_loop(0, ids.shape[0], step, jnp.int32(0), unroll=4)


def asked(lay, ids, pos):
    return pl.pallas_call(
        functools.partial(asked_kernel, lay),
        out_shape=i32(USED + 1),
        in_specs=[SMEM, SMEM],
        out_specs=SMEM,
        scratch_shapes=[pltpu.SMEM((2 * lay.stored,), jnp.int32)],
        name="asked",
    )(ids, pos)


def pick_kernel(lay, stages, pieces, spots, stored_ref, *rest):
    parts, outs = rest[: len(stages)], rest[len(stages) :]
    size = USED // pieces
    for piece, out in enumerate(outs):
        for n in range(size):
            q = spots[piece * size + n] - lay.stored
            value = stored_ref[jnp.minimum(q + lay.stored, lay.stored - 1)]
            for s, part in zip(stages, parts):
                at = jnp.clip(q - lay.start[s], 0, lay.size(s) - 1)
                value = jnp.where(q >= lay.start[s], part[at], value)
            out[n] = value


def pick(lay, stages, pieces, spots, stored, parts, name):
    block = stored.shape[-1]
    return pl.pallas_call(
        functools.partial(pick_kernel, lay, stages, pieces),
        out_shape=(jax.ShapeDtypeStruct((USED // pieces, block, block), stored.dtype),) * pieces,
        in_specs=[SMEM, VMEM] + [VMEM] * len(parts),
        out_specs=(VMEM,) * pieces,
        compiler_params=params(16),
        name=name,
    )(spots, stored, *parts)


def multiply(count, entry, left, right, acc):
    spare = acc.shape[0] - 1

    def group(g, carry):
        found = []
        for u in range(UNROLL):
            p = g * UNROLL + u
            i, j, o = entry(p)
            o = jnp.where(p < count, o, spare)
            found.append((o, jnp.dot(left[i], right[j], preferred_element_type=jnp.float32)))
        for o, term in found:
            acc[o] += term
        return carry

    lax.fori_loop(0, (count + UNROLL - 1) // UNROLL, group, 0)


def own_kernel(lay, prods, plan, counts, pos, stored_ref, *rest):
    parts = rest[: len(lay.stages)]
    acc, panel, sem = rest[len(lay.stages) :]
    copies = [pltpu.make_async_copy(stored_ref, panel.at[pl.ds(0, lay.stored)], sem.at[0])]
    for s, part in enumerate(parts):
        copies.append(
            pltpu.make_async_copy(
                part.at[pl.ds(0, lay.size(s))], panel.at[pl.ds(lay.stored + lay.start[s], lay.size(s))], sem.at[s + 1]
            )
        )
    for copy in copies:
        copy.start()

    def zero(o, carry):
        acc[o] = jnp.zeros(acc.shape[1:], acc.dtype)
        return carry

    lax.fori_loop(0, acc.shape[0], zero, 0)
    for copy in copies:
        copy.wait()

    def where(which):
        lower = which >= lay.stored
        return jnp.where(lower, lay.stored + pos[jnp.where(lower, which - lay.stored, 0)], which)

    def entry(p):
        return where(plan[0, 0, p]), where(plan[1, 0, p]), plan[2, 0, p]

    multiply(counts[0], entry, panel, panel, acc)


def own_section(lay, plan, counts, pos, stored, parts):
    block = stored.shape[-1]
    prods = plan.shape[2]
    return pl.pallas_call(
        functools.partial(own_kernel, lay, prods),
        out_shape=jax.ShapeDtypeStruct((OUTSLOTS + 1, block, block), jnp.float32),
        in_specs=[SMEM, SMEM, SMEM, VMEM] + [VMEM] * len(parts),
        out_specs=VMEM,
        scratch_shapes=[
            pltpu.VMEM((lay.stored + lay.total, block, block), stored.dtype),
            pltpu.SemaphoreType.DMA((len(parts) + 1,)),
        ],
        compiler_params=params(20),
        cost_estimate=cost(0.01),
        name="own_section",
    )(plan, counts, pos, stored, *parts)


def places_kernel(lay, late, plan, counts, slots_l, slots_r, pos, pos_r, asked_r, out, spots):
    for n in range(USED):
        spots[n] = panel_place(lay, pos, asked_r[n])
    own_from, own_to = lay.start[lay.self_stage], lay.start[lay.self_stage + 1]
    late_from = lay.start[late[0]]

    def step(p, carry):
        left_id, right_id = plan[0, 1, p], plan[1, 1, p]
        lower = left_id >= lay.stored
        q = pos[jnp.where(lower, left_id - lay.stored, 0)]
        out[0, p] = jnp.where(lower & (q >= own_from) & (q < own_to), USED + q - own_from, slots_l[p])
        lower = right_id >= lay.stored
        q = pos_r[jnp.where(lower, right_id - lay.stored, 0)]
        out[1, p] = jnp.where(lower & (q >= late_from), USED + q - late_from, slots_r[p])
        out[2, p] = jnp.where(p < counts[1], plan[2, 1, p], OUTSLOTS)
        return carry

    lax.fori_loop(0, plan.shape[2], step, 0, unroll=4)


def places(lay, late, plan, counts, slots_l, slots_r, pos, pos_r, asked_r):
    return pl.pallas_call(
        functools.partial(places_kernel, lay, late),
        out_shape=(i32(3, plan.shape[2]), i32(USED)),
        in_specs=[SMEM] * 7,
        out_specs=(SMEM, SMEM),
        name="places",
    )(plan, counts, slots_l, slots_r, pos, pos_r, asked_r)


def either(n, first, first_size, others):
    value = first[jnp.minimum(n, first_size - 1)]
    at = first_size
    for part, size in others:
        value = jnp.where(n >= at, part[jnp.clip(n - at, 0, size - 1)], value)
        at += size
    return value


def next_kernel(lay, late, token, spots, counts, old, self_ref, left, right, *rest):
    parts, (acc, out) = rest[:-2], rest[-2:]
    lefts = [(self_ref, lay.size(lay.self_stage))]
    rights = [(part, lay.size(s)) for s, part in zip(late, parts)]

    def group(g, carry):
        found = []
        for u in range(NEXT_UNROLL):
            p = g * NEXT_UNROLL + u
            i, j, o = spots[0, p], spots[1, p], spots[2, p]
            a = either(i, left, USED, lefts)
            b = either(j, right, USED, rights)
            found.append((o, jnp.dot(a, b, preferred_element_type=jnp.float32)))
        for o, term in found:
            acc[o] += term
        return carry

    lax.fori_loop(0, (counts[1] + NEXT_UNROLL - 1) // NEXT_UNROLL, group, 0)
    for o in range(OUTSLOTS):
        out[o] = acc[o].astype(out.dtype)


def next_section(lay, late, token, spots, counts, acc, self_part, left, right, parts):
    block = self_part.shape[-1]
    return pl.pallas_call(
        functools.partial(next_kernel, lay, late),
        out_shape=(
            jax.ShapeDtypeStruct(acc.shape, acc.dtype),
            jax.ShapeDtypeStruct((OUTSLOTS, block, block), self_part.dtype),
        ),
        in_specs=[SMEM] * 3 + [VMEM] * (4 + len(parts)),
        out_specs=(VMEM, VMEM),
        input_output_aliases={3: 0},
        compiler_params=params(20),
        cost_estimate=cost(0.01),
        name="next_section",
    )(token, spots, counts, acc, self_part, left, right, *parts)[1]


FLIGHT = 2
EARLY = 6


def body(upper_blocks, block_targets, product_plan, live_counts):
    stored = upper_blocks[0, 0]
    targets = block_targets[0, 0]
    counts = live_counts[0, 0]
    plan = jnp.transpose(product_plan[0, 0], (2, 0, 1))
    prods = plan.shape[2]
    lay = Layout(stored.shape[0], lax.axis_size("col"))
    stages = list(range(len(lay.stages)))
    early, late = stages[:EARLY], stages[EARLY:]
    col = lax.axis_index("col").astype(jnp.int32).reshape(1)

    def exchange(s, send):
        if len(lay.stages[s]) == 1:
            return moved(send, "col", lay.stages[s][0])
        parts = [
            moved(send[n * lay.cap : (n + 1) * lay.cap], "col", d) for n, d in enumerate(lay.stages[s])
        ]
        return jnp.concatenate(parts, axis=0)

    order = Order(col)
    sends = list(order.gate(first_stage(lay, targets, col, stored)))
    got = [exchange(s, sends[s]) for s in range(FIRST)]
    *rest, pos = rest_stages(lay, targets, col, plan, order.gate(stored))
    sends += rest
    got += [exchange(s, sends[s]) for s in stages[FIRST:-1]]
    for s in stages[:2]:
        got[s] = order.gate(got[s])
    reqs_r, slots_l, slots_r = order.gate(wanted(2 * lay.stored, order.gate(plan), prods))
    asked_r = moved(reqs_r, "row", 1)
    pos_r = moved(pos, "row", -1)
    asked_r, pos_r = order.gate((asked_r, pos_r))
    spots, asked_r = order.gate(places(lay, late, order.gate(plan), counts, slots_l, slots_r, pos, pos_r, asked_r))
    got[2] = order.gate(got[2])
    got[3] = order.gate(got[3])
    rows = prods // stored.shape[-1]
    ids = got[lay.self_stage][-1, : 16 * rows : 16].reshape(-1).astype(jnp.int32)
    asked_l = order.gate(asked(lay, order.gate(ids), pos))
    for s in stages[4:-1]:
        got[s] = order.gate(got[s])
    got.append(exchange(stages[-1], order.gate(sends[-1])))
    picked = order.gate(pick(lay, early, RIGHT_PIECES, asked_r, stored, [got[s] for s in early], "pick_right"))
    right = [moved(piece, "row", -1) for piece in picked]
    got[-1] = order.gate(got[-1])
    forwarded = [moved(got[s], "row", -1) for s in late]
    ready = [s for s in stages if s != lay.self_stage]
    picked = pick(lay, ready, LEFT_PIECES, order.gate(asked_l), stored, [got[s] for s in ready], "pick_left")
    left = [moved(piece, "col", -1) for piece in order.gate(picked)]
    acc = own_section(lay, plan, counts, pos, stored, got)
    out = next_section(lay, late, order.token, spots, counts, acc, sends[lay.self_stage], *left, *right, forwarded)
    return out[None, None]


def solution(mesh):
    placed = (
        P("row", "col", None, None, None),
        P("row", "col", None),
        P("row", "col", None, None, None),
        P("row", "col", None),
    )
    return jax.shard_map(
        body,
        mesh=mesh,
        in_specs=placed,
        out_specs=P("row", "col", None, None, None),
        check_vma=False,
    )
```

```python
import functools

import jax
import jax.numpy as jnp
from jax import lax
from jax.experimental import pallas as pl
from jax.experimental.pallas import tpu as pltpu
from jax.sharding import PartitionSpec as P

OUTSLOTS = 32
USED = 24
UNROLL = 16
NEXT_UNROLL = 32
FIRST = 1
LEFT_PIECES = 1
RIGHT_PIECES = 1
FIRST_MIB = 61
MIB = 1 << 20

SMEM = pl.BlockSpec(memory_space=pltpu.SMEM)
VMEM = pl.BlockSpec(memory_space=pltpu.VMEM)
HBM = pl.BlockSpec(memory_space=pltpu.HBM)


def cost(us):
    return pl.CostEstimate(flops=0, bytes_accessed=int(us * 3.5e6), transcendentals=0)


def i32(*shape):
    return jax.ShapeDtypeStruct(shape, jnp.int32)


def params(mib):
    return pltpu.CompilerParams(vmem_limit_bytes=mib * MIB)


def moved(value, axis, steps):
    count = lax.axis_size(axis)
    return lax.ppermute(value, axis, [(s, (s + steps) % count) for s in range(count)])


def after(value, *needed):
    return lax.optimization_barrier((value, *needed))[0]


class Order:
    def __init__(self, token):
        self.token = token

    def gate(self, value):
        value, self.token = lax.optimization_barrier((value, self.token))
        return value


class Layout:
    def __init__(self, stored, cols):
        self.stored = stored
        self.cols = cols
        self.cap = (stored + cols - 2) // (cols - 1)
        half = cols // 2
        others = [d for d in range(2, cols) if d != half]
        others.sort(key=lambda d: (half - abs(d - half), d))
        others = others[1:2] + others[:1] + others[2:3] + others[3:]
        pieces = min(5, len(others))
        cuts = [len(others) * i // pieces for i in range(pieces + 1)]
        groups = [others[a:b] for a, b in zip(cuts, cuts[1:])]
        self.stages = groups[:1] + [[1]] + groups[1:] + [[half]]
        self.base = [0] * cols
        self.start = []
        at = 0
        for stage in self.stages:
            self.start.append(at)
            for d in stage:
                self.base[d] = at
                at += self.cap
        self.total = at
        self.start.append(at)
        self.self_stage = self.stages.index([1])

    def size(self, s):
        return self.start[s + 1] - self.start[s]


def offset_of(lay, tgt, k, me):
    d = tgt[k] - me
    return jnp.where(d < 0, d + lay.cols, d)


def first_kernel(lay, tgt, col, stored_ref, *rest):
    outs, (buf, found, sem) = rest[:FIRST], rest[FIRST:]
    goals = []
    for n, offset in enumerate(d for stage in lay.stages[:FIRST] for d in stage):
        goal = col[0] + offset
        goals.append(jnp.where(goal >= lay.cols, goal - lay.cols, goal))
    at = [jnp.int32(n * lay.cap) for n in range(len(goals))]
    for k in range(lay.stored):
        target = tgt[k]
        for n, goal in enumerate(goals):
            hit = target == goal
            found[jnp.where(hit, at[n], lay.total)] = k
            at[n] = at[n] + hit.astype(jnp.int32)
    total = lay.start[FIRST]
    for j in range(total):
        pltpu.make_async_copy(stored_ref.at[found[j]], buf.at[j], sem).start()
    pltpu.make_async_copy(buf, buf, sem).wait()
    for s, out in enumerate(outs):
        for j in range(lay.size(s)):
            out[j] = buf[lay.start[s] + j].T


def first_stage(lay, targets, col, stored):
    block = stored.shape[-1]
    return pl.pallas_call(
        functools.partial(first_kernel, lay),
        out_shape=tuple(jax.ShapeDtypeStruct((lay.size(s), block, block), stored.dtype) for s in range(FIRST)),
        in_specs=[SMEM, SMEM, HBM],
        out_specs=(VMEM,) * FIRST,
        scratch_shapes=[
            pltpu.VMEM((lay.start[FIRST], block, block), stored.dtype),
            pltpu.SMEM((lay.total + 1,), jnp.int32),
            pltpu.SemaphoreType.DMA,
        ],
        compiler_params=params(FIRST_MIB),
        name="first_stage",
    )(targets, col, stored)


def rest_kernel(lay, tgt, col, plan, stored_ref, *rest):
    outs, pos, inv, cnt = rest[:-3], rest[-3], rest[-2], rest[-1]
    for d in range(lay.cols):
        cnt[d] = lay.base[d]

    def place(k, carry):
        d = offset_of(lay, tgt, k, col[0])
        q = cnt[d]
        cnt[d] = q + 1
        pos[k] = q
        inv[q] = k
        return carry

    lax.fori_loop(0, lay.stored, place, 0)
    for s in range(FIRST, len(lay.stages)):

        def flip(j, carry, s=s):
            outs[s - FIRST][j] = stored_ref[inv[lay.start[s] + j]].T
            return carry

        lax.fori_loop(0, lay.size(s), flip, 0, unroll=9 if lay.size(s) % 9 == 0 else 1)
    note = outs[lay.self_stage - FIRST]
    block = note.shape[-1]
    for row in range(plan.shape[2] // block):
        line = plan[0, 1:2, row * block : row * block + block].astype(jnp.float32)
        note[lay.size(lay.self_stage), row * 16 : row * 16 + 16, :] = jnp.broadcast_to(line, (16, block)).astype(note.dtype)


def rest_stages(lay, targets, col, plan, stored):
    block = stored.shape[-1]
    shapes = tuple(
        jax.ShapeDtypeStruct((lay.size(s) + (s == lay.self_stage), block, block), stored.dtype)
        for s in range(FIRST, len(lay.stages))
    )
    return pl.pallas_call(
        functools.partial(rest_kernel, lay),
        out_shape=shapes + (i32(lay.stored),),
        in_specs=[SMEM, SMEM, VMEM, VMEM],
        out_specs=(VMEM,) * len(shapes) + (SMEM,),
        scratch_shapes=[pltpu.SMEM((lay.total,), jnp.int32), pltpu.SMEM((lay.cols,), jnp.int32)],
        compiler_params=params(12),
        cost_estimate=cost(0.01),
        name="rest_stages",
    )(targets, col, plan, stored)


def wanted_kernel(prods, plan, reqs_r, slots_l, slots_r, seen_l, seen_r):
    def clear(i, carry):
        seen_l[i] = -1
        seen_r[i] = -1
        return carry

    lax.fori_loop(0, seen_l.shape[0], clear, 0, unroll=6 if seen_l.shape[0] % 6 == 0 else 1)
    for i in range(USED):
        reqs_r[i] = 0

    def step(p, counts):
        sides = ((slots_l, seen_l), (slots_r, seen_r))
        found = [plan[side, 1, p] for side in range(2)]
        known = [seen[which] for (_, seen), which in zip(sides, found)]
        slot = [jnp.where(k < 0, n, k) for k, n in zip(known, counts)]
        for (slots, seen), which, at in zip(sides, found, slot):
            seen[which] = at
            slots[p] = at
        reqs_r[slot[1]] = found[1]
        return tuple(n + (k < 0).astype(jnp.int32) for k, n in zip(known, counts))

    lax.fori_loop(0, prods, step, (jnp.int32(0), jnp.int32(0)), unroll=4)


def wanted(panel_size, plan, prods):
    return pl.pallas_call(
        functools.partial(wanted_kernel, prods),
        out_shape=(i32(USED), i32(prods), i32(prods)),
        in_specs=[SMEM],
        out_specs=(SMEM,) * 3,
        scratch_shapes=[pltpu.SMEM((panel_size,), jnp.int32)] * 2,
        cost_estimate=cost(0.01),
        name="wanted",
    )(plan)


def panel_place(lay, pos, which):
    lower = which >= lay.stored
    return jnp.where(lower, lay.stored + pos[jnp.where(lower, which - lay.stored, 0)], which)


def asked_kernel(lay, ids, pos, spots, seen):
    def clear(i, carry):
        seen[i] = 0
        return carry

    lax.fori_loop(0, seen.shape[0], clear, 0, unroll=6 if seen.shape[0] % 6 == 0 else 1)

    def step(p, n):
        which = ids[p]
        known = seen[which]
        spots[n] = panel_place(lay, pos, which)
        seen[which] = 1
        return n + 1 - known

    lax.fori_loop(0, ids.shape[0], step, jnp.int32(0), unroll=4)


def asked(lay, ids, pos):
    return pl.pallas_call(
        functools.partial(asked_kernel, lay),
        out_shape=i32(USED + 1),
        in_specs=[SMEM, SMEM],
        out_specs=SMEM,
        scratch_shapes=[pltpu.SMEM((2 * lay.stored,), jnp.int32)],
        name="asked",
    )(ids, pos)


def pick_kernel(lay, stages, pieces, spots, stored_ref, *rest):
    parts, outs = rest[: len(stages)], rest[len(stages) :]
    size = USED // pieces
    for piece, out in enumerate(outs):
        for n in range(size):
            q = spots[piece * size + n] - lay.stored
            value = stored_ref[jnp.minimum(q + lay.stored, lay.stored - 1)]
            for s, part in zip(stages, parts):
                at = jnp.clip(q - lay.start[s], 0, lay.size(s) - 1)
                value = jnp.where(q >= lay.start[s], part[at], value)
            out[n] = value


def pick(lay, stages, pieces, spots, stored, parts, name):
    block = stored.shape[-1]
    return pl.pallas_call(
        functools.partial(pick_kernel, lay, stages, pieces),
        out_shape=(jax.ShapeDtypeStruct((USED // pieces, block, block), stored.dtype),) * pieces,
        in_specs=[SMEM, VMEM] + [VMEM] * len(parts),
        out_specs=(VMEM,) * pieces,
        compiler_params=params(16),
        name=name,
    )(spots, stored, *parts)


def multiply(count, entry, left, right, acc):
    spare = acc.shape[0] - 1

    def group(g, carry):
        found = []
        for u in range(UNROLL):
            p = g * UNROLL + u
            i, j, o = entry(p)
            o = jnp.where(p < count, o, spare)
            found.append((o, jnp.dot(left[i], right[j], preferred_element_type=jnp.float32)))
        for o, term in found:
            acc[o] += term
        return carry

    lax.fori_loop(0, (count + UNROLL - 1) // UNROLL, group, 0)


def own_kernel(lay, prods, plan, counts, pos, stored_ref, *rest):
    parts = rest[: len(lay.stages)]
    acc, panel, sem = rest[len(lay.stages) :]
    copies = [pltpu.make_async_copy(stored_ref, panel.at[pl.ds(0, lay.stored)], sem.at[0])]
    for s, part in enumerate(parts):
        copies.append(
            pltpu.make_async_copy(
                part.at[pl.ds(0, lay.size(s))], panel.at[pl.ds(lay.stored + lay.start[s], lay.size(s))], sem.at[s + 1]
            )
        )
    for copy in copies:
        copy.start()

    def zero(o, carry):
        acc[o] = jnp.zeros(acc.shape[1:], acc.dtype)
        return carry

    lax.fori_loop(0, acc.shape[0], zero, 0)
    for copy in copies:
        copy.wait()

    def where(which):
        lower = which >= lay.stored
        return jnp.where(lower, lay.stored + pos[jnp.where(lower, which - lay.stored, 0)], which)

    def entry(p):
        return where(plan[0, 0, p]), where(plan[1, 0, p]), plan[2, 0, p]

    multiply(counts[0], entry, panel, panel, acc)


def own_section(lay, plan, counts, pos, stored, parts):
    block = stored.shape[-1]
    prods = plan.shape[2]
    return pl.pallas_call(
        functools.partial(own_kernel, lay, prods),
        out_shape=jax.ShapeDtypeStruct((OUTSLOTS + 1, block, block), jnp.float32),
        in_specs=[SMEM, SMEM, SMEM, VMEM] + [VMEM] * len(parts),
        out_specs=VMEM,
        scratch_shapes=[
            pltpu.VMEM((lay.stored + lay.total, block, block), stored.dtype),
            pltpu.SemaphoreType.DMA((len(parts) + 1,)),
        ],
        compiler_params=params(20),
        cost_estimate=cost(0.01),
        name="own_section",
    )(plan, counts, pos, stored, *parts)


def places_kernel(lay, late, plan, counts, slots_l, slots_r, pos, pos_r, asked_r, out, spots):
    for n in range(USED):
        spots[n] = panel_place(lay, pos, asked_r[n])
    own_from, own_to = lay.start[lay.self_stage], lay.start[lay.self_stage + 1]
    late_from = lay.start[late[0]]

    def step(p, carry):
        left_id, right_id = plan[0, 1, p], plan[1, 1, p]
        lower = left_id >= lay.stored
        q = pos[jnp.where(lower, left_id - lay.stored, 0)]
        out[0, p] = jnp.where(lower & (q >= own_from) & (q < own_to), USED + q - own_from, slots_l[p])
        lower = right_id >= lay.stored
        q = pos_r[jnp.where(lower, right_id - lay.stored, 0)]
        out[1, p] = jnp.where(lower & (q >= late_from), USED + q - late_from, slots_r[p])
        out[2, p] = jnp.where(p < counts[1], plan[2, 1, p], OUTSLOTS)
        return carry

    lax.fori_loop(0, plan.shape[2], step, 0, unroll=4)


def places(lay, late, plan, counts, slots_l, slots_r, pos, pos_r, asked_r):
    return pl.pallas_call(
        functools.partial(places_kernel, lay, late),
        out_shape=(i32(3, plan.shape[2]), i32(USED)),
        in_specs=[SMEM] * 7,
        out_specs=(SMEM, SMEM),
        name="places",
    )(plan, counts, slots_l, slots_r, pos, pos_r, asked_r)


def either(n, first, first_size, others):
    value = first[jnp.minimum(n, first_size - 1)]
    at = first_size
    for part, size in others:
        value = jnp.where(n >= at, part[jnp.clip(n - at, 0, size - 1)], value)
        at += size
    return value


def next_kernel(lay, late, token, spots, counts, old, self_ref, left, right, *rest):
    parts, (out, acc) = rest[:-2], rest[-2:]
    for o in range(OUTSLOTS + 1):
        acc[o] = old[o]
    lefts = [(self_ref, lay.size(lay.self_stage))]
    rights = [(part, lay.size(s)) for s, part in zip(late, parts)]

    def group(g, carry):
        found = []
        for u in range(NEXT_UNROLL):
            p = g * NEXT_UNROLL + u
            i, j, o = spots[0, p], spots[1, p], spots[2, p]
            a = either(i, left, USED, lefts)
            b = either(j, right, USED, rights)
            found.append((o, jnp.dot(a, b, preferred_element_type=jnp.float32)))
        for o, term in found:
            acc[o] += term
        return carry

    lax.fori_loop(0, (counts[1] + NEXT_UNROLL - 1) // NEXT_UNROLL, group, 0)
    for o in range(OUTSLOTS):
        out[o] = acc[o].astype(out.dtype)


def next_section(lay, late, token, spots, counts, acc, self_part, left, right, parts):
    block = self_part.shape[-1]
    return pl.pallas_call(
        functools.partial(next_kernel, lay, late),
        out_shape=jax.ShapeDtypeStruct((OUTSLOTS, block, block), self_part.dtype),
        in_specs=[SMEM] * 3 + [VMEM] * (4 + len(parts)),
        out_specs=VMEM,
        scratch_shapes=[pltpu.VMEM(acc.shape, acc.dtype)],
        compiler_params=params(20),
        cost_estimate=cost(0.01),
        name="next_section",
    )(token, spots, counts, acc, self_part, left, right, *parts)


FLIGHT = 2
EARLY = 6


def body(upper_blocks, block_targets, product_plan, live_counts):
    stored = upper_blocks[0, 0]
    targets = block_targets[0, 0]
    counts = live_counts[0, 0]
    plan = jnp.transpose(product_plan[0, 0], (2, 0, 1))
    prods = plan.shape[2]
    lay = Layout(stored.shape[0], lax.axis_size("col"))
    stages = list(range(len(lay.stages)))
    early, late = stages[:EARLY], stages[EARLY:]
    col = lax.axis_index("col").astype(jnp.int32).reshape(1)

    def exchange(s, send):
        if len(lay.stages[s]) == 1:
            return moved(send, "col", lay.stages[s][0])
        parts = [
            moved(send[n * lay.cap : (n + 1) * lay.cap], "col", d) for n, d in enumerate(lay.stages[s])
        ]
        return jnp.concatenate(parts, axis=0)

    order = Order(col)
    sends = list(order.gate(first_stage(lay, targets, col, stored)))
    got = [exchange(s, sends[s]) for s in range(FIRST)]
    *rest, pos = rest_stages(lay, targets, col, plan, order.gate(stored))
    sends += rest
    got += [exchange(s, sends[s]) for s in stages[FIRST:-1]]
    for s in stages[:2]:
        got[s] = order.gate(got[s])
    reqs_r, slots_l, slots_r = order.gate(wanted(2 * lay.stored, order.gate(plan), prods))
    asked_r = moved(reqs_r, "row", 1)
    pos_r = moved(pos, "row", -1)
    asked_r, pos_r = order.gate((asked_r, pos_r))
    spots, asked_r = order.gate(places(lay, late, order.gate(plan), counts, slots_l, slots_r, pos, pos_r, asked_r))
    got[2] = order.gate(got[2])
    got[3] = order.gate(got[3])
    rows = prods // stored.shape[-1]
    ids = got[lay.self_stage][-1, : 16 * rows : 16].reshape(-1).astype(jnp.int32)
    asked_l = order.gate(asked(lay, order.gate(ids), pos))
    for s in stages[4:-1]:
        got[s] = order.gate(got[s])
    got.append(exchange(stages[-1], order.gate(sends[-1])))
    picked = order.gate(pick(lay, early, RIGHT_PIECES, asked_r, stored, [got[s] for s in early], "pick_right"))
    right = [moved(piece, "row", -1) for piece in picked]
    got[-1] = order.gate(got[-1])
    forwarded = [moved(got[s], "row", -1) for s in late]
    ready = [s for s in stages if s != lay.self_stage]
    picked = pick(lay, ready, LEFT_PIECES, order.gate(asked_l), stored, [got[s] for s in ready], "pick_left")
    left = [moved(piece, "col", -1) for piece in order.gate(picked)]
    acc = own_section(lay, plan, counts, pos, stored, got)
    out = next_section(lay, late, order.token, spots, counts, acc, sends[lay.self_stage], *left, *right, forwarded)
    return out[None, None]


def solution(mesh):
    placed = (
        P("row", "col", None, None, None),
        P("row", "col", None),
        P("row", "col", None, None, None),
        P("row", "col", None),
    )
    return jax.shard_map(
        body,
        mesh=mesh,
        in_specs=placed,
        out_specs=P("row", "col", None, None, None),
        check_vma=False,
    )
```

```python
import functools

import jax
import jax.numpy as jnp
from jax import lax
from jax.experimental import pallas as pl
from jax.experimental.pallas import tpu as pltpu
from jax.sharding import PartitionSpec as P

OUTSLOTS = 32
USED = 24
UNROLL = 16
NEXT_UNROLL = 32
FIRST = 1
LEFT_PIECES = 1
RIGHT_PIECES = 1
FIRST_MIB = 61
MIB = 1 << 20

SMEM = pl.BlockSpec(memory_space=pltpu.SMEM)
VMEM = pl.BlockSpec(memory_space=pltpu.VMEM)
HBM = pl.BlockSpec(memory_space=pltpu.HBM)


def cost(us):
    return pl.CostEstimate(flops=0, bytes_accessed=int(us * 3.5e6), transcendentals=0)


def i32(*shape):
    return jax.ShapeDtypeStruct(shape, jnp.int32)


def params(mib):
    return pltpu.CompilerParams(vmem_limit_bytes=mib * MIB)


def moved(value, axis, steps):
    count = lax.axis_size(axis)
    return lax.ppermute(value, axis, [(s, (s + steps) % count) for s in range(count)])


def after(value, *needed):
    return lax.optimization_barrier((value, *needed))[0]


class Order:
    def __init__(self, token):
        self.token = token

    def gate(self, value):
        value, self.token = lax.optimization_barrier((value, self.token))
        return value


class Layout:
    def __init__(self, stored, cols):
        self.stored = stored
        self.cols = cols
        self.cap = (stored + cols - 2) // (cols - 1)
        half = cols // 2
        others = [d for d in range(2, cols) if d != half]
        others.sort(key=lambda d: (half - abs(d - half), d))
        others = others[1:2] + others[:1] + others[2:3] + others[3:]
        pieces = min(5, len(others))
        cuts = [len(others) * i // pieces for i in range(pieces + 1)]
        groups = [others[a:b] for a, b in zip(cuts, cuts[1:])]
        self.stages = groups[:1] + [[1]] + groups[1:] + [[half]]
        self.base = [0] * cols
        self.start = []
        at = 0
        for stage in self.stages:
            self.start.append(at)
            for d in stage:
                self.base[d] = at
                at += self.cap
        self.total = at
        self.start.append(at)
        self.self_stage = self.stages.index([1])

    def size(self, s):
        return self.start[s + 1] - self.start[s]


def offset_of(lay, tgt, k, me):
    d = tgt[k] - me
    return jnp.where(d < 0, d + lay.cols, d)


def first_kernel(lay, tgt, col, stored_ref, *rest):
    outs, (buf, found, sem) = rest[:FIRST], rest[FIRST:]
    goals = []
    for n, offset in enumerate(d for stage in lay.stages[:FIRST] for d in stage):
        goal = col[0] + offset
        goals.append(jnp.where(goal >= lay.cols, goal - lay.cols, goal))
    at = [jnp.int32(n * lay.cap) for n in range(len(goals))]
    for k in range(lay.stored):
        target = tgt[k]
        for n, goal in enumerate(goals):
            hit = target == goal
            found[jnp.where(hit, at[n], lay.total)] = k
            at[n] = at[n] + hit.astype(jnp.int32)
    total = lay.start[FIRST]
    copies = [pltpu.make_async_copy(stored_ref.at[found[j]], buf.at[j], sem.at[j]) for j in range(total)]
    for copy in copies:
        copy.start()
    for s, out in enumerate(outs):
        for j in range(lay.size(s)):
            copies[lay.start[s] + j].wait()
            out[j] = buf[lay.start[s] + j].T


def first_stage(lay, targets, col, stored):
    block = stored.shape[-1]
    return pl.pallas_call(
        functools.partial(first_kernel, lay),
        out_shape=tuple(jax.ShapeDtypeStruct((lay.size(s), block, block), stored.dtype) for s in range(FIRST)),
        in_specs=[SMEM, SMEM, HBM],
        out_specs=(VMEM,) * FIRST,
        scratch_shapes=[
            pltpu.VMEM((lay.start[FIRST], block, block), stored.dtype),
            pltpu.SMEM((lay.total + 1,), jnp.int32),
            pltpu.SemaphoreType.DMA((lay.start[FIRST],)),
        ],
        compiler_params=params(FIRST_MIB),
        name="first_stage",
    )(targets, col, stored)


def rest_kernel(lay, tgt, col, plan, stored_ref, *rest):
    outs, pos, inv, cnt = rest[:-3], rest[-3], rest[-2], rest[-1]
    for d in range(lay.cols):
        cnt[d] = lay.base[d]

    def place(k, carry):
        d = offset_of(lay, tgt, k, col[0])
        q = cnt[d]
        cnt[d] = q + 1
        pos[k] = q
        inv[q] = k
        return carry

    lax.fori_loop(0, lay.stored, place, 0)
    for s in range(FIRST, len(lay.stages)):

        def flip(j, carry, s=s):
            outs[s - FIRST][j] = stored_ref[inv[lay.start[s] + j]].T
            return carry

        lax.fori_loop(0, lay.size(s), flip, 0, unroll=9 if lay.size(s) % 9 == 0 else 1)
    note = outs[lay.self_stage - FIRST]
    block = note.shape[-1]
    for row in range(plan.shape[2] // block):
        line = plan[0, 1:2, row * block : row * block + block].astype(jnp.float32)
        note[lay.size(lay.self_stage), row * 16 : row * 16 + 16, :] = jnp.broadcast_to(line, (16, block)).astype(note.dtype)


def rest_stages(lay, targets, col, plan, stored):
    block = stored.shape[-1]
    shapes = tuple(
        jax.ShapeDtypeStruct((lay.size(s) + (s == lay.self_stage), block, block), stored.dtype)
        for s in range(FIRST, len(lay.stages))
    )
    return pl.pallas_call(
        functools.partial(rest_kernel, lay),
        out_shape=shapes + (i32(lay.stored),),
        in_specs=[SMEM, SMEM, VMEM, VMEM],
        out_specs=(VMEM,) * len(shapes) + (SMEM,),
        scratch_shapes=[pltpu.SMEM((lay.total,), jnp.int32), pltpu.SMEM((lay.cols,), jnp.int32)],
        compiler_params=params(12),
        cost_estimate=cost(0.01),
        name="rest_stages",
    )(targets, col, plan, stored)


def wanted_kernel(prods, plan, reqs_r, slots_l, slots_r, seen_l, seen_r):
    def clear(i, carry):
        seen_l[i] = -1
        seen_r[i] = -1
        return carry

    lax.fori_loop(0, seen_l.shape[0], clear, 0, unroll=6 if seen_l.shape[0] % 6 == 0 else 1)
    for i in range(USED):
        reqs_r[i] = 0

    def step(p, counts):
        sides = ((slots_l, seen_l), (slots_r, seen_r))
        found = [plan[side, 1, p] for side in range(2)]
        known = [seen[which] for (_, seen), which in zip(sides, found)]
        slot = [jnp.where(k < 0, n, k) for k, n in zip(known, counts)]
        for (slots, seen), which, at in zip(sides, found, slot):
            seen[which] = at
            slots[p] = at
        reqs_r[slot[1]] = found[1]
        return tuple(n + (k < 0).astype(jnp.int32) for k, n in zip(known, counts))

    lax.fori_loop(0, prods, step, (jnp.int32(0), jnp.int32(0)), unroll=4)


def wanted(panel_size, plan, prods):
    return pl.pallas_call(
        functools.partial(wanted_kernel, prods),
        out_shape=(i32(USED), i32(prods), i32(prods)),
        in_specs=[SMEM],
        out_specs=(SMEM,) * 3,
        scratch_shapes=[pltpu.SMEM((panel_size,), jnp.int32)] * 2,
        cost_estimate=cost(0.01),
        name="wanted",
    )(plan)


def panel_place(lay, pos, which):
    lower = which >= lay.stored
    return jnp.where(lower, lay.stored + pos[jnp.where(lower, which - lay.stored, 0)], which)


def asked_kernel(lay, ids, pos, spots, seen):
    def clear(i, carry):
        seen[i] = 0
        return carry

    lax.fori_loop(0, seen.shape[0], clear, 0, unroll=6 if seen.shape[0] % 6 == 0 else 1)

    def step(p, n):
        which = ids[p]
        known = seen[which]
        spots[n] = panel_place(lay, pos, which)
        seen[which] = 1
        return n + 1 - known

    lax.fori_loop(0, ids.shape[0], step, jnp.int32(0), unroll=4)


def asked(lay, ids, pos):
    return pl.pallas_call(
        functools.partial(asked_kernel, lay),
        out_shape=i32(USED + 1),
        in_specs=[SMEM, SMEM],
        out_specs=SMEM,
        scratch_shapes=[pltpu.SMEM((2 * lay.stored,), jnp.int32)],
        name="asked",
    )(ids, pos)


def pick_kernel(lay, stages, pieces, spots, stored_ref, *rest):
    parts, outs = rest[: len(stages)], rest[len(stages) :]
    size = USED // pieces
    for piece, out in enumerate(outs):
        for n in range(size):
            q = spots[piece * size + n] - lay.stored
            value = stored_ref[jnp.minimum(q + lay.stored, lay.stored - 1)]
            for s, part in zip(stages, parts):
                at = jnp.clip(q - lay.start[s], 0, lay.size(s) - 1)
                value = jnp.where(q >= lay.start[s], part[at], value)
            out[n] = value


def pick(lay, stages, pieces, spots, stored, parts, name):
    block = stored.shape[-1]
    return pl.pallas_call(
        functools.partial(pick_kernel, lay, stages, pieces),
        out_shape=(jax.ShapeDtypeStruct((USED // pieces, block, block), stored.dtype),) * pieces,
        in_specs=[SMEM, VMEM] + [VMEM] * len(parts),
        out_specs=(VMEM,) * pieces,
        compiler_params=params(16),
        name=name,
    )(spots, stored, *parts)


def multiply(count, entry, left, right, acc):
    spare = acc.shape[0] - 1

    def group(g, carry):
        found = []
        for u in range(UNROLL):
            p = g * UNROLL + u
            i, j, o = entry(p)
            o = jnp.where(p < count, o, spare)
            found.append((o, jnp.dot(left[i], right[j], preferred_element_type=jnp.float32)))
        for o, term in found:
            acc[o] += term
        return carry

    lax.fori_loop(0, (count + UNROLL - 1) // UNROLL, group, 0)


def own_kernel(lay, prods, plan, counts, pos, stored_ref, *rest):
    parts = rest[: len(lay.stages)]
    acc, panel, sem = rest[len(lay.stages) :]
    copies = [pltpu.make_async_copy(stored_ref, panel.at[pl.ds(0, lay.stored)], sem.at[0])]
    for s, part in enumerate(parts):
        copies.append(
            pltpu.make_async_copy(
                part.at[pl.ds(0, lay.size(s))], panel.at[pl.ds(lay.stored + lay.start[s], lay.size(s))], sem.at[s + 1]
            )
        )
    for copy in copies:
        copy.start()

    def zero(o, carry):
        acc[o] = jnp.zeros(acc.shape[1:], acc.dtype)
        return carry

    lax.fori_loop(0, acc.shape[0], zero, 0)
    for copy in copies:
        copy.wait()

    def where(which):
        lower = which >= lay.stored
        return jnp.where(lower, lay.stored + pos[jnp.where(lower, which - lay.stored, 0)], which)

    def entry(p):
        return where(plan[0, 0, p]), where(plan[1, 0, p]), plan[2, 0, p]

    multiply(counts[0], entry, panel, panel, acc)


def own_section(lay, plan, counts, pos, stored, parts):
    block = stored.shape[-1]
    prods = plan.shape[2]
    return pl.pallas_call(
        functools.partial(own_kernel, lay, prods),
        out_shape=jax.ShapeDtypeStruct((OUTSLOTS + 1, block, block), jnp.float32),
        in_specs=[SMEM, SMEM, SMEM, VMEM] + [VMEM] * len(parts),
        out_specs=VMEM,
        scratch_shapes=[
            pltpu.VMEM((lay.stored + lay.total, block, block), stored.dtype),
            pltpu.SemaphoreType.DMA((len(parts) + 1,)),
        ],
        compiler_params=params(20),
        cost_estimate=cost(0.01),
        name="own_section",
    )(plan, counts, pos, stored, *parts)


def places_kernel(lay, late, plan, counts, slots_l, slots_r, pos, pos_r, asked_r, out, spots):
    for n in range(USED):
        spots[n] = panel_place(lay, pos, asked_r[n])
    own_from, own_to = lay.start[lay.self_stage], lay.start[lay.self_stage + 1]
    late_from = lay.start[late[0]]

    def step(p, carry):
        left_id, right_id = plan[0, 1, p], plan[1, 1, p]
        lower = left_id >= lay.stored
        q = pos[jnp.where(lower, left_id - lay.stored, 0)]
        out[0, p] = jnp.where(lower & (q >= own_from) & (q < own_to), USED + q - own_from, slots_l[p])
        lower = right_id >= lay.stored
        q = pos_r[jnp.where(lower, right_id - lay.stored, 0)]
        out[1, p] = jnp.where(lower & (q >= late_from), USED + q - late_from, slots_r[p])
        out[2, p] = jnp.where(p < counts[1], plan[2, 1, p], OUTSLOTS)
        return carry

    lax.fori_loop(0, plan.shape[2], step, 0, unroll=4)


def places(lay, late, plan, counts, slots_l, slots_r, pos, pos_r, asked_r):
    return pl.pallas_call(
        functools.partial(places_kernel, lay, late),
        out_shape=(i32(3, plan.shape[2]), i32(USED)),
        in_specs=[SMEM] * 7,
        out_specs=(SMEM, SMEM),
        name="places",
    )(plan, counts, slots_l, slots_r, pos, pos_r, asked_r)


def either(n, first, first_size, others):
    value = first[jnp.minimum(n, first_size - 1)]
    at = first_size
    for part, size in others:
        value = jnp.where(n >= at, part[jnp.clip(n - at, 0, size - 1)], value)
        at += size
    return value


def next_kernel(lay, late, token, spots, counts, old, self_ref, left, right, *rest):
    parts, (out, acc) = rest[:-2], rest[-2:]
    for o in range(OUTSLOTS + 1):
        acc[o] = old[o]
    lefts = [(self_ref, lay.size(lay.self_stage))]
    rights = [(part, lay.size(s)) for s, part in zip(late, parts)]

    def group(g, carry):
        found = []
        for u in range(NEXT_UNROLL):
            p = g * NEXT_UNROLL + u
            i, j, o = spots[0, p], spots[1, p], spots[2, p]
            a = either(i, left, USED, lefts)
            b = either(j, right, USED, rights)
            found.append((o, jnp.dot(a, b, preferred_element_type=jnp.float32)))
        for o, term in found:
            acc[o] += term
        return carry

    lax.fori_loop(0, (counts[1] + NEXT_UNROLL - 1) // NEXT_UNROLL, group, 0)
    for o in range(OUTSLOTS):
        out[o] = acc[o].astype(out.dtype)


def next_section(lay, late, token, spots, counts, acc, self_part, left, right, parts):
    block = self_part.shape[-1]
    return pl.pallas_call(
        functools.partial(next_kernel, lay, late),
        out_shape=jax.ShapeDtypeStruct((OUTSLOTS, block, block), self_part.dtype),
        in_specs=[SMEM] * 3 + [VMEM] * (4 + len(parts)),
        out_specs=VMEM,
        scratch_shapes=[pltpu.VMEM(acc.shape, acc.dtype)],
        compiler_params=params(20),
        cost_estimate=cost(0.01),
        name="next_section",
    )(token, spots, counts, acc, self_part, left, right, *parts)


FLIGHT = 2
EARLY = 6


def body(upper_blocks, block_targets, product_plan, live_counts):
    stored = upper_blocks[0, 0]
    targets = block_targets[0, 0]
    counts = live_counts[0, 0]
    plan = jnp.transpose(product_plan[0, 0], (2, 0, 1))
    prods = plan.shape[2]
    lay = Layout(stored.shape[0], lax.axis_size("col"))
    stages = list(range(len(lay.stages)))
    early, late = stages[:EARLY], stages[EARLY:]
    col = lax.axis_index("col").astype(jnp.int32).reshape(1)

    def exchange(s, send):
        if len(lay.stages[s]) == 1:
            return moved(send, "col", lay.stages[s][0])
        parts = [
            moved(send[n * lay.cap : (n + 1) * lay.cap], "col", d) for n, d in enumerate(lay.stages[s])
        ]
        return jnp.concatenate(parts, axis=0)

    order = Order(col)
    sends = list(order.gate(first_stage(lay, targets, col, stored)))
    got = [exchange(s, sends[s]) for s in range(FIRST)]
    *rest, pos = rest_stages(lay, targets, col, plan, order.gate(stored))
    sends += rest
    got += [exchange(s, sends[s]) for s in stages[FIRST:-1]]
    for s in stages[:2]:
        got[s] = order.gate(got[s])
    reqs_r, slots_l, slots_r = order.gate(wanted(2 * lay.stored, order.gate(plan), prods))
    asked_r = moved(reqs_r, "row", 1)
    pos_r = moved(pos, "row", -1)
    asked_r, pos_r = order.gate((asked_r, pos_r))
    spots, asked_r = order.gate(places(lay, late, order.gate(plan), counts, slots_l, slots_r, pos, pos_r, asked_r))
    got[2] = order.gate(got[2])
    got[3] = order.gate(got[3])
    rows = prods // stored.shape[-1]
    ids = got[lay.self_stage][-1, : 16 * rows : 16].reshape(-1).astype(jnp.int32)
    asked_l = order.gate(asked(lay, order.gate(ids), pos))
    for s in stages[4:-1]:
        got[s] = order.gate(got[s])
    got.append(exchange(stages[-1], order.gate(sends[-1])))
    picked = order.gate(pick(lay, early, RIGHT_PIECES, asked_r, stored, [got[s] for s in early], "pick_right"))
    right = [moved(piece, "row", -1) for piece in picked]
    got[-1] = order.gate(got[-1])
    forwarded = [moved(got[s], "row", -1) for s in late]
    ready = [s for s in stages if s != lay.self_stage]
    picked = pick(lay, ready, LEFT_PIECES, order.gate(asked_l), stored, [got[s] for s in ready], "pick_left")
    left = [moved(piece, "col", -1) for piece in order.gate(picked)]
    acc = own_section(lay, plan, counts, pos, stored, got)
    out = next_section(lay, late, order.token, spots, counts, acc, sends[lay.self_stage], *left, *right, forwarded)
    return out[None, None]


def solution(mesh):
    placed = (
        P("row", "col", None, None, None),
        P("row", "col", None),
        P("row", "col", None, None, None),
        P("row", "col", None),
    )
    return jax.shard_map(
        body,
        mesh=mesh,
        in_specs=placed,
        out_specs=P("row", "col", None, None, None),
        check_vma=False,
    )
```

```python
import functools

import jax
import jax.numpy as jnp
from jax import lax
from jax.experimental import pallas as pl
from jax.experimental.pallas import tpu as pltpu
from jax.sharding import PartitionSpec as P

OUTSLOTS = 32
USED = 24
UNROLL = 16
NEXT_UNROLL = 32
FIRST = 1
LEFT_PIECES = 1
RIGHT_PIECES = 1
FIRST_MIB = 61
MIB = 1 << 20

SMEM = pl.BlockSpec(memory_space=pltpu.SMEM)
VMEM = pl.BlockSpec(memory_space=pltpu.VMEM)
HBM = pl.BlockSpec(memory_space=pltpu.HBM)


def cost(us):
    return pl.CostEstimate(flops=0, bytes_accessed=int(us * 3.5e6), transcendentals=0)


def i32(*shape):
    return jax.ShapeDtypeStruct(shape, jnp.int32)


def params(mib):
    return pltpu.CompilerParams(vmem_limit_bytes=mib * MIB)


def moved(value, axis, steps):
    count = lax.axis_size(axis)
    return lax.ppermute(value, axis, [(s, (s + steps) % count) for s in range(count)])


def after(value, *needed):
    return lax.optimization_barrier((value, *needed))[0]


class Order:
    def __init__(self, token):
        self.token = token

    def gate(self, value):
        value, self.token = lax.optimization_barrier((value, self.token))
        return value


class Layout:
    def __init__(self, stored, cols):
        self.stored = stored
        self.cols = cols
        self.cap = (stored + cols - 2) // (cols - 1)
        half = cols // 2
        others = [d for d in range(2, cols) if d != half]
        others.sort(key=lambda d: (half - abs(d - half), d))
        others = others[1:2] + others[:1] + others[2:3] + others[3:]
        pieces = min(5, len(others))
        cuts = [len(others) * i // pieces for i in range(pieces + 1)]
        groups = [others[a:b] for a, b in zip(cuts, cuts[1:])]
        self.stages = groups[:1] + [[1]] + groups[1:] + [[half]]
        self.base = [0] * cols
        self.start = []
        at = 0
        for stage in self.stages:
            self.start.append(at)
            for d in stage:
                self.base[d] = at
                at += self.cap
        self.total = at
        self.start.append(at)
        self.self_stage = self.stages.index([1])

    def size(self, s):
        return self.start[s + 1] - self.start[s]


def offset_of(lay, tgt, k, me):
    d = tgt[k] - me
    return jnp.where(d < 0, d + lay.cols, d)


def first_kernel(lay, tgt, col, stored_ref, *rest):
    outs, (buf, found, sem) = rest[:FIRST], rest[FIRST:]
    goals = []
    for n, offset in enumerate(d for stage in lay.stages[:FIRST] for d in stage):
        goal = col[0] + offset
        goals.append(jnp.where(goal >= lay.cols, goal - lay.cols, goal))

    def find(k, at):
        hits = [tgt[k] == goal for goal in goals]
        for n, hit in enumerate(hits):
            found[jnp.where(hit, at[n], lay.total)] = k
        return tuple(n + hit.astype(jnp.int32) for n, hit in zip(at, hits))

    starts = tuple(jnp.int32(n * lay.cap) for n in range(len(goals)))
    lax.fori_loop(0, lay.stored, find, starts, unroll=9 if lay.stored % 9 == 0 else 1)

    def fetch(j, carry):
        pltpu.make_async_copy(stored_ref.at[found[j]], buf.at[j], sem).start()
        return carry

    lax.fori_loop(0, lay.start[FIRST], fetch, 0)
    pltpu.make_async_copy(buf, buf, sem).wait()
    for s, out in enumerate(outs):

        def flip(j, carry, s=s, out=out):
            out[j] = buf[lay.start[s] + j].T
            return carry

        lax.fori_loop(0, lay.size(s), flip, 0, unroll=3 if lay.size(s) % 3 == 0 else 1)


def first_stage(lay, targets, col, stored):
    block = stored.shape[-1]
    return pl.pallas_call(
        functools.partial(first_kernel, lay),
        out_shape=tuple(jax.ShapeDtypeStruct((lay.size(s), block, block), stored.dtype) for s in range(FIRST)),
        in_specs=[SMEM, SMEM, HBM],
        out_specs=(VMEM,) * FIRST,
        scratch_shapes=[
            pltpu.VMEM((lay.start[FIRST], block, block), stored.dtype),
            pltpu.SMEM((lay.total + 1,), jnp.int32),
            pltpu.SemaphoreType.DMA,
        ],
        compiler_params=params(FIRST_MIB),
        name="first_stage",
    )(targets, col, stored)


def rest_kernel(lay, tgt, col, plan, stored_ref, *rest):
    outs, pos, inv, cnt = rest[:-3], rest[-3], rest[-2], rest[-1]
    for d in range(lay.cols):
        cnt[d] = lay.base[d]

    def place(k, carry):
        d = offset_of(lay, tgt, k, col[0])
        q = cnt[d]
        cnt[d] = q + 1
        pos[k] = q
        inv[q] = k
        return carry

    lax.fori_loop(0, lay.stored, place, 0)
    for s in range(FIRST, len(lay.stages)):

        def flip(j, carry, s=s):
            outs[s - FIRST][j] = stored_ref[inv[lay.start[s] + j]].T
            return carry

        lax.fori_loop(0, lay.size(s), flip, 0, unroll=9 if lay.size(s) % 9 == 0 else 1)
    note = outs[lay.self_stage - FIRST]
    block = note.shape[-1]
    for row in range(plan.shape[2] // block):
        line = plan[0, 1:2, row * block : row * block + block].astype(jnp.float32)
        note[lay.size(lay.self_stage), row * 16 : row * 16 + 16, :] = jnp.broadcast_to(line, (16, block)).astype(note.dtype)


def rest_stages(lay, targets, col, plan, stored):
    block = stored.shape[-1]
    shapes = tuple(
        jax.ShapeDtypeStruct((lay.size(s) + (s == lay.self_stage), block, block), stored.dtype)
        for s in range(FIRST, len(lay.stages))
    )
    return pl.pallas_call(
        functools.partial(rest_kernel, lay),
        out_shape=shapes + (i32(lay.stored),),
        in_specs=[SMEM, SMEM, VMEM, VMEM],
        out_specs=(VMEM,) * len(shapes) + (SMEM,),
        scratch_shapes=[pltpu.SMEM((lay.total,), jnp.int32), pltpu.SMEM((lay.cols,), jnp.int32)],
        compiler_params=params(12),
        cost_estimate=cost(0.01),
        name="rest_stages",
    )(targets, col, plan, stored)


def wanted_kernel(prods, plan, reqs_r, slots_l, slots_r, seen_l, seen_r):
    def clear(i, carry):
        seen_l[i] = -1
        seen_r[i] = -1
        return carry

    lax.fori_loop(0, seen_l.shape[0], clear, 0, unroll=6 if seen_l.shape[0] % 6 == 0 else 1)
    for i in range(USED):
        reqs_r[i] = 0

    def step(p, counts):
        sides = ((slots_l, seen_l), (slots_r, seen_r))
        found = [plan[side, 1, p] for side in range(2)]
        known = [seen[which] for (_, seen), which in zip(sides, found)]
        slot = [jnp.where(k < 0, n, k) for k, n in zip(known, counts)]
        for (slots, seen), which, at in zip(sides, found, slot):
            seen[which] = at
            slots[p] = at
        reqs_r[slot[1]] = found[1]
        return tuple(n + (k < 0).astype(jnp.int32) for k, n in zip(known, counts))

    lax.fori_loop(0, prods, step, (jnp.int32(0), jnp.int32(0)), unroll=4)


def wanted(panel_size, plan, prods):
    return pl.pallas_call(
        functools.partial(wanted_kernel, prods),
        out_shape=(i32(USED), i32(prods), i32(prods)),
        in_specs=[SMEM],
        out_specs=(SMEM,) * 3,
        scratch_shapes=[pltpu.SMEM((panel_size,), jnp.int32)] * 2,
        cost_estimate=cost(0.01),
        name="wanted",
    )(plan)


def panel_place(lay, pos, which):
    lower = which >= lay.stored
    return jnp.where(lower, lay.stored + pos[jnp.where(lower, which - lay.stored, 0)], which)


def asked_kernel(lay, ids, pos, spots, seen):
    def clear(i, carry):
        seen[i] = 0
        return carry

    lax.fori_loop(0, seen.shape[0], clear, 0, unroll=6 if seen.shape[0] % 6 == 0 else 1)

    def step(p, n):
        which = ids[p]
        known = seen[which]
        spots[n] = panel_place(lay, pos, which)
        seen[which] = 1
        return n + 1 - known

    lax.fori_loop(0, ids.shape[0], step, jnp.int32(0), unroll=4)


def asked(lay, ids, pos):
    return pl.pallas_call(
        functools.partial(asked_kernel, lay),
        out_shape=i32(USED + 1),
        in_specs=[SMEM, SMEM],
        out_specs=SMEM,
        scratch_shapes=[pltpu.SMEM((2 * lay.stored,), jnp.int32)],
        name="asked",
    )(ids, pos)


def pick_kernel(lay, stages, pieces, spots, stored_ref, *rest):
    parts, outs = rest[: len(stages)], rest[len(stages) :]
    size = USED // pieces
    for piece, out in enumerate(outs):
        for n in range(size):
            q = spots[piece * size + n] - lay.stored
            value = stored_ref[jnp.minimum(q + lay.stored, lay.stored - 1)]
            for s, part in zip(stages, parts):
                at = jnp.clip(q - lay.start[s], 0, lay.size(s) - 1)
                value = jnp.where(q >= lay.start[s], part[at], value)
            out[n] = value


def pick(lay, stages, pieces, spots, stored, parts, name):
    block = stored.shape[-1]
    return pl.pallas_call(
        functools.partial(pick_kernel, lay, stages, pieces),
        out_shape=(jax.ShapeDtypeStruct((USED // pieces, block, block), stored.dtype),) * pieces,
        in_specs=[SMEM, VMEM] + [VMEM] * len(parts),
        out_specs=(VMEM,) * pieces,
        compiler_params=params(16),
        name=name,
    )(spots, stored, *parts)


def multiply(count, entry, left, right, acc):
    spare = acc.shape[0] - 1

    def group(g, carry):
        found = []
        for u in range(UNROLL):
            p = g * UNROLL + u
            i, j, o = entry(p)
            o = jnp.where(p < count, o, spare)
            found.append((o, jnp.dot(left[i], right[j], preferred_element_type=jnp.float32)))
        for o, term in found:
            acc[o] += term
        return carry

    lax.fori_loop(0, (count + UNROLL - 1) // UNROLL, group, 0)


def own_kernel(lay, prods, plan, counts, pos, stored_ref, *rest):
    parts = rest[: len(lay.stages)]
    acc, panel, sem = rest[len(lay.stages) :]
    copies = [pltpu.make_async_copy(stored_ref, panel.at[pl.ds(0, lay.stored)], sem.at[0])]
    for s, part in enumerate(parts):
        copies.append(
            pltpu.make_async_copy(
                part.at[pl.ds(0, lay.size(s))], panel.at[pl.ds(lay.stored + lay.start[s], lay.size(s))], sem.at[s + 1]
            )
        )
    for copy in copies:
        copy.start()

    def zero(o, carry):
        acc[o] = jnp.zeros(acc.shape[1:], acc.dtype)
        return carry

    lax.fori_loop(0, acc.shape[0], zero, 0)
    for copy in copies:
        copy.wait()

    def where(which):
        lower = which >= lay.stored
        return jnp.where(lower, lay.stored + pos[jnp.where(lower, which - lay.stored, 0)], which)

    def entry(p):
        return where(plan[0, 0, p]), where(plan[1, 0, p]), plan[2, 0, p]

    multiply(counts[0], entry, panel, panel, acc)


def own_section(lay, plan, counts, pos, stored, parts):
    block = stored.shape[-1]
    prods = plan.shape[2]
    return pl.pallas_call(
        functools.partial(own_kernel, lay, prods),
        out_shape=jax.ShapeDtypeStruct((OUTSLOTS + 1, block, block), jnp.float32),
        in_specs=[SMEM, SMEM, SMEM, VMEM] + [VMEM] * len(parts),
        out_specs=VMEM,
        scratch_shapes=[
            pltpu.VMEM((lay.stored + lay.total, block, block), stored.dtype),
            pltpu.SemaphoreType.DMA((len(parts) + 1,)),
        ],
        compiler_params=params(20),
        cost_estimate=cost(0.01),
        name="own_section",
    )(plan, counts, pos, stored, *parts)


def places_kernel(lay, late, plan, counts, slots_l, slots_r, pos, pos_r, asked_r, out, spots):
    for n in range(USED):
        spots[n] = panel_place(lay, pos, asked_r[n])
    own_from, own_to = lay.start[lay.self_stage], lay.start[lay.self_stage + 1]
    late_from = lay.start[late[0]]

    def step(p, carry):
        left_id, right_id = plan[0, 1, p], plan[1, 1, p]
        lower = left_id >= lay.stored
        q = pos[jnp.where(lower, left_id - lay.stored, 0)]
        out[0, p] = jnp.where(lower & (q >= own_from) & (q < own_to), USED + q - own_from, slots_l[p])
        lower = right_id >= lay.stored
        q = pos_r[jnp.where(lower, right_id - lay.stored, 0)]
        out[1, p] = jnp.where(lower & (q >= late_from), USED + q - late_from, slots_r[p])
        out[2, p] = jnp.where(p < counts[1], plan[2, 1, p], OUTSLOTS)
        return carry

    lax.fori_loop(0, plan.shape[2], step, 0, unroll=4)


def places(lay, late, plan, counts, slots_l, slots_r, pos, pos_r, asked_r):
    return pl.pallas_call(
        functools.partial(places_kernel, lay, late),
        out_shape=(i32(3, plan.shape[2]), i32(USED)),
        in_specs=[SMEM] * 7,
        out_specs=(SMEM, SMEM),
        name="places",
    )(plan, counts, slots_l, slots_r, pos, pos_r, asked_r)


def either(n, first, first_size, others):
    value = first[jnp.minimum(n, first_size - 1)]
    at = first_size
    for part, size in others:
        value = jnp.where(n >= at, part[jnp.clip(n - at, 0, size - 1)], value)
        at += size
    return value


def next_kernel(lay, late, token, spots, counts, old, self_ref, left, right, *rest):
    parts, (out, acc) = rest[:-2], rest[-2:]
    for o in range(OUTSLOTS + 1):
        acc[o] = old[o]
    lefts = [(self_ref, lay.size(lay.self_stage))]
    rights = [(part, lay.size(s)) for s, part in zip(late, parts)]

    def group(g, carry):
        found = []
        for u in range(NEXT_UNROLL):
            p = g * NEXT_UNROLL + u
            i, j, o = spots[0, p], spots[1, p], spots[2, p]
            a = either(i, left, USED, lefts)
            b = either(j, right, USED, rights)
            found.append((o, jnp.dot(a, b, preferred_element_type=jnp.float32)))
        for o, term in found:
            acc[o] += term
        return carry

    lax.fori_loop(0, (counts[1] + NEXT_UNROLL - 1) // NEXT_UNROLL, group, 0)
    for o in range(OUTSLOTS):
        out[o] = acc[o].astype(out.dtype)


def next_section(lay, late, token, spots, counts, acc, self_part, left, right, parts):
    block = self_part.shape[-1]
    return pl.pallas_call(
        functools.partial(next_kernel, lay, late),
        out_shape=jax.ShapeDtypeStruct((OUTSLOTS, block, block), self_part.dtype),
        in_specs=[SMEM] * 3 + [VMEM] * (4 + len(parts)),
        out_specs=VMEM,
        scratch_shapes=[pltpu.VMEM(acc.shape, acc.dtype)],
        compiler_params=params(20),
        cost_estimate=cost(0.01),
        name="next_section",
    )(token, spots, counts, acc, self_part, left, right, *parts)


FLIGHT = 2
EARLY = 6


def body(upper_blocks, block_targets, product_plan, live_counts):
    stored = upper_blocks[0, 0]
    targets = block_targets[0, 0]
    counts = live_counts[0, 0]
    plan = jnp.transpose(product_plan[0, 0], (2, 0, 1))
    prods = plan.shape[2]
    lay = Layout(stored.shape[0], lax.axis_size("col"))
    stages = list(range(len(lay.stages)))
    early, late = stages[:EARLY], stages[EARLY:]
    col = lax.axis_index("col").astype(jnp.int32).reshape(1)

    def exchange(s, send):
        if len(lay.stages[s]) == 1:
            return moved(send, "col", lay.stages[s][0])
        parts = [
            moved(send[n * lay.cap : (n + 1) * lay.cap], "col", d) for n, d in enumerate(lay.stages[s])
        ]
        return jnp.concatenate(parts, axis=0)

    order = Order(col)
    sends = list(order.gate(first_stage(lay, targets, col, stored)))
    got = [exchange(s, sends[s]) for s in range(FIRST)]
    *rest, pos = rest_stages(lay, targets, col, plan, order.gate(stored))
    sends += rest
    got += [exchange(s, sends[s]) for s in stages[FIRST:-1]]
    for s in stages[:2]:
        got[s] = order.gate(got[s])
    reqs_r, slots_l, slots_r = order.gate(wanted(2 * lay.stored, order.gate(plan), prods))
    asked_r = moved(reqs_r, "row", 1)
    pos_r = moved(pos, "row", -1)
    asked_r, pos_r = order.gate((asked_r, pos_r))
    spots, asked_r = order.gate(places(lay, late, order.gate(plan), counts, slots_l, slots_r, pos, pos_r, asked_r))
    got[2] = order.gate(got[2])
    got[3] = order.gate(got[3])
    rows = prods // stored.shape[-1]
    ids = got[lay.self_stage][-1, : 16 * rows : 16].reshape(-1).astype(jnp.int32)
    asked_l = order.gate(asked(lay, order.gate(ids), pos))
    for s in stages[4:-1]:
        got[s] = order.gate(got[s])
    got.append(exchange(stages[-1], order.gate(sends[-1])))
    picked = order.gate(pick(lay, early, RIGHT_PIECES, asked_r, stored, [got[s] for s in early], "pick_right"))
    right = [moved(piece, "row", -1) for piece in picked]
    got[-1] = order.gate(got[-1])
    forwarded = [moved(got[s], "row", -1) for s in late]
    ready = [s for s in stages if s != lay.self_stage]
    picked = pick(lay, ready, LEFT_PIECES, order.gate(asked_l), stored, [got[s] for s in ready], "pick_left")
    left = [moved(piece, "col", -1) for piece in order.gate(picked)]
    acc = own_section(lay, plan, counts, pos, stored, got)
    out = next_section(lay, late, order.token, spots, counts, acc, sends[lay.self_stage], *left, *right, forwarded)
    return out[None, None]


def solution(mesh):
    placed = (
        P("row", "col", None, None, None),
        P("row", "col", None),
        P("row", "col", None, None, None),
        P("row", "col", None),
    )
    return jax.shard_map(
        body,
        mesh=mesh,
        in_specs=placed,
        out_specs=P("row", "col", None, None, None),
        check_vma=False,
    )
```
